128 devices in a mesh: wave: 32 (over x, z, core), lat: 4 (over y).
Axes of the slice: x: 4, y: 4, z: 4, core: 2. Of those that a mesh axis runs over, the one named last changes fastest.
Arguments:
- spectra: bfloat16 [1280, 1280, 128], P('wave', 'lat'), may hold values from -0.1796875 to 0.1796875
- legendre: bfloat16 [1280, 1280, 128], P('wave', 'lat'), may hold values from -0.25 to 0.25
- wave_list: int32 [1280], replicated, may hold values from 0 to 1279, as said below
- cycle_lons: int32 [128], replicated, may hold values from 20 to 5136, as said below
Outputs:
- grid_out: bfloat16 [128, 5632, 64], P('lat', 'wave')
The draws below stay inside these ranges and needn't reach their ends.
Inputs may be any that keep to these rules, and one draw needn't show every extreme that they name: `wave_list`: A permutation of the wavenumbers; the 1280 // 32 slots of each index of wave hold whole pairs m and 1279 - m. `cycle_lons`: window rows run from north to south, one row from each run of 20 Gaussian latitudes; a row on latitude cycle i counted from the nearer pole has 20 + 4 i longitudes. The first row is on cycle 0 and some row is on the equator's cycle.
All inputs are finite; a program needn't handle non-finite values.
Results may differ from the reference program's by a relative error of at most 0.015.
Values may be sent and summed in bfloat16 or wider, within the bound.
A program may use at most 64 MiB of HBM per device.

```python
import math
import jax
import jax.numpy as jnp
from jax import lax

M = 1280
F = 64
NLW = 128
NLAT = 2560
STRIDE = 20
NLONP = 5632
N_LAT = 4


def draw_wave_list(key, part):
    key = jax.random.fold_in(key, 11)
    pair_order = jax.random.permutation(key, M // 2).astype(jnp.int32)
    slot_index = jnp.arange(M, dtype=jnp.int32)
    chosen = pair_order[slot_index // 2]
    return jnp.where(slot_index % 2 == 0, chosen, M - 1 - chosen).astype(jnp.int32)


def draw_cycle_lons(key, part):
    key = jax.random.fold_in(key, 23)
    row_index = jnp.arange(NLW, dtype=jnp.int32)
    jitter = jax.random.randint(key, (NLW,), 0, STRIDE, dtype=jnp.int32)
    pinned = (row_index == 0) | (row_index == NLAT // 2 // STRIDE)
    jitter = jnp.where(pinned, 0, jitter)
    latitude = STRIDE * row_index + jitter
    cycle_number = jnp.minimum(latitude, NLAT - 1 - latitude)
    return (20 + 4 * cycle_number).astype(jnp.int32)


def strengthened(array, own_key, source, target, shards_of, factor):
    owner, partner = [(jnp.arange(array.shape[dim]) // (array.shape[dim] // shards_of)).reshape([-1 if axis == dim else 1 for axis in range(array.ndim)]) for dim in (source, target)]
    chosen = jax.random.permutation(own_key, shards_of)[partner]
    strong = (owner == chosen) | (owner == (partner + shards_of // 2) % shards_of)
    return jnp.where(strong, factor * array, array)


def block_scale(stream_key, extent, cuts, least, top_value):
    gain, own = 1.0, jax.random.fold_in(stream_key, 6)
    for axis_at, blocks in cuts:
        draws = jnp.exp(jax.random.uniform(jax.random.fold_in(own, axis_at), (blocks,), jnp.float32, least / len(cuts), top_value / len(cuts)))
        gain = gain * jnp.repeat(draws, extent[axis_at] // blocks).reshape([-1 if axis == axis_at else 1 for axis in range(len(extent))])
    return gain


def gaussian(own_key, dims, width, reach, cuts=(), held_as=jnp.bfloat16):
    array = jax.random.normal(own_key, dims, jnp.float32) * width
    if len(cuts) > 0:
        array = block_scale(own_key, dims, cuts, -0.22, 0.18) * array
    return jnp.clip(array, min=-reach, max=reach).astype(held_as)


def noise_with(key, dims, deviation, limit, pieces, heavy, kind=jnp.bfloat16):
    result = deviation * jax.random.normal(key, dims, jnp.float32)
    if pieces:
        result = result * block_scale(key, dims, pieces, -0.22, 0.18)
    return jnp.clip(strengthened(result, jax.random.fold_in(key, 3), *heavy), -limit, limit).astype(kind)


def setup_inputs(seed: int = 0) -> dict:
    streams_of = jax.random.split(jax.random.key(seed), 5)
    spectra = gaussian(streams_of[0], (M, M, 2 * F), 0.03, 0.1796875, ((0, 32), (1, 4)))
    legendre = noise_with(streams_of[1], (M, M, NLW), M ** -0.5, 0.25, ((0, 32), (1, 4)), (1, 2, 4, 2.0))
    wave_list = draw_wave_list(jax.random.fold_in(streams_of[4], 71), 0)
    cycle_lons = draw_cycle_lons(jax.random.fold_in(streams_of[4], 71), 0)
    return {"spectra": spectra, "legendre": legendre, "wave_list": wave_list, "cycle_lons": cycle_lons}


TWO_PI = 2.0 * math.pi
BLOCK = 512


def lon_block_table(wave_numbers, row_lons, k_first, k_count):
    k_index = k_first + jnp.arange(k_count, dtype=jnp.int32)
    turn_index = (k_index[:, None] * wave_numbers[None, :]) % row_lons
    angles = turn_index.astype(jnp.float32) * (TWO_PI / row_lons.astype(jnp.float32))
    weights = jnp.where(wave_numbers == 0, 1.0, jnp.where(2 * wave_numbers < row_lons, 2.0, 0.0)).astype(jnp.float32)
    scales = jnp.where((k_index < row_lons)[:, None], weights[None, :], 0.0).astype(jnp.float32)
    cosine_part = (scales * jnp.cos(angles)).astype(jnp.bfloat16)
    sine_part = (scales * (-jnp.sin(angles))).astype(jnp.bfloat16)
    return jnp.concatenate([cosine_part, sine_part], 1)


def reference(spectra, legendre, wave_list, cycle_lons):
    block_depth = M // N_LAT
    offsets = jnp.arange(M, dtype=jnp.int32)

    def one_slot(args):
        spec_rows, leg_rows, wave_number = args
        live_mask = (offsets < M - wave_number)[:, None]
        masked = jnp.where(live_mask, spec_rows, jnp.zeros_like(spec_rows))
        partials = jnp.einsum('qjw,qjc->qwc', leg_rows.reshape(N_LAT, block_depth, -1).astype(jnp.float32), masked.reshape(N_LAT, block_depth, -1).astype(jnp.float32))
        rounded = lax.optimization_barrier(partials.astype(jnp.bfloat16))
        return jnp.sum(rounded.astype(jnp.float32), 0).astype(jnp.bfloat16)

    fourier = lax.map(one_slot, (spectra, legendre, wave_list))

    def one_row(args):
        fourier_row, row_lons = args
        stacked = jnp.concatenate([fourier_row[:, :F], fourier_row[:, F:]], 0)

        def lon_block(k_first):
            table = lon_block_table(wave_list, row_lons, k_first, BLOCK)
            return jnp.dot(table, stacked, preferred_element_type=jnp.float32)

        starts = jnp.arange(NLONP // BLOCK, dtype=jnp.int32) * BLOCK
        return lax.map(lon_block, starts).reshape(NLONP, F).astype(jnp.bfloat16)

    return lax.map(one_row, (jnp.transpose(fourier, (1, 0, 2)), cycle_lons))
```

```python
import jax
import jax.numpy as jnp
from jax import lax
from jax.experimental import pallas as pl
from jax.experimental.pallas import tpu as pltpu
from jax.sharding import PartitionSpec as P

M = 1280
F = 64
NLW = 128
NLAT = 2560
STRIDE = 20
NLONP = 5632
N_WAVE = 32
N_LAT = 4

SLOTS = M // N_WAVE
DEPTH = M // N_LAT
BAND = NLW // N_LAT
LONS = NLONP // N_WAVE
HALF = LONS // 2
LANES = 128
QUADS = N_WAVE // 4
GROUPS = ((0, 24), (24, 16))

COS_TERMS = (
    0.999999009718151, -19.738932854525416, 64.92691787698224,
    -85.24978872544477, 58.68039930519758, -20.879193249375327,
)
SIN_TERMS = (
    6.283184816484557, -41.34156560570182, 81.59907809153451,
    -76.60361308658534, 41.288123420059144, -12.375788874464046,
)


def cos_sin(product, two_lons, inverse):
    turns = jnp.floor(product * inverse + 0.5)
    u = (product - turns * two_lons) * inverse
    z = u * u
    c = jnp.full_like(z, COS_TERMS[-1])
    for term in COS_TERMS[-2::-1]:
        c = c * z + term
    s = jnp.full_like(z, SIN_TERMS[-1])
    for term in SIN_TERMS[-2::-1]:
        s = s * z + term
    return c, s * u


def kernel(waves_s, lons_s, waves_v, spectra, legendre, raw, *scratch):
    names = iter(scratch)
    spec, leg, partial = next(names), next(names), next(names)
    bands, from_dn, from_up, sum_dn, sum_up, mine, got, coef, table = (
        [next(names) for _ in GROUPS] for _ in range(9)
    )
    acc, out, m_nat, m_grp, c0, s0, c1, s1 = (next(names) for _ in range(8))
    in_sem, y_send, y_recv, a_send, a_recv, o_send, o_recv, own_sem = names

    me = lax.axis_index("wave")
    lat = lax.axis_index("lat")
    up = lax.rem(lat + 1, N_LAT)
    dn = lax.rem(lat + N_LAT - 1, N_LAT)
    opp = lax.rem(lat + 2, N_LAT)
    row = lat * BAND + me

    def most_lons(w):
        first = STRIDE * w + STRIDE - 1
        last = NLAT - 1 - STRIDE * w
        return 20 + 4 * jnp.minimum(first, last)

    def peer(step):
        return lax.rem(me + step, N_WAVE)

    def load(g, which):
        off, size = GROUPS[g]
        source, target = ((spectra, spec), (legendre, leg))[which]
        return pltpu.make_async_copy(
            source.at[pl.ds(off, size)], target.at[pl.ds(off, size)], in_sem.at[g, which]
        )

    for g in range(len(GROUPS)):
        for which in range(2):
            load(g, which).start()

    barrier = pltpu.get_barrier_semaphore()
    for other in (up, dn):
        pl.semaphore_signal(
            barrier, inc=1, device_id={"wave": me, "lat": other}, device_id_type=pl.DeviceIdType.MESH
        )

    def greet(step, carry):
        pl.semaphore_signal(
            barrier, inc=1, device_id={"wave": peer(step), "lat": lat},
            device_id_type=pl.DeviceIdType.MESH,
        )
        return carry

    lax.fori_loop(1, N_WAVE, greet, 0)

    def along_y(g, at, source, target, other):
        return pltpu.make_async_remote_copy(
            src_ref=source, dst_ref=target, send_sem=y_send.at[g, at], recv_sem=y_recv.at[g, at],
            device_id={"wave": me, "lat": other}, device_id_type=pl.DeviceIdType.MESH,
        )

    def y_copies(g):
        half = BAND // 2 * GROUPS[g][1]
        lo, hi = pl.ds(0, half), pl.ds(half, half)
        b = bands[g]
        return (
            along_y(g, 0, b.at[opp, lo], from_dn[g], up),
            along_y(g, 1, b.at[opp, hi], from_up[g], dn),
            along_y(g, 2, b.at[up, hi], sum_dn[g].at[hi], up),
            along_y(g, 3, b.at[dn, lo], sum_up[g].at[lo], dn),
            along_y(g, 4, b.at[up, lo], sum_dn[g].at[lo], up),
            along_y(g, 5, b.at[dn, hi], sum_up[g].at[hi], dn),
        )

    def legendre_sums(g):
        off, size = GROUPS[g]
        load(g, 0).wait()
        load(g, 1).wait()

        def slot(s, carry):
            live = M - waves_s[me * SLOTS + off + s] - lat * DEPTH
            offsets = lax.broadcasted_iota(jnp.int32, (DEPTH, LANES), 0)
            masked = jnp.where(offsets < live, spec[off + s].astype(jnp.float32), 0.0)
            partial[pl.ds(pl.multiple_of(s * NLW, NLW), NLW), :] = lax.dot_general(
                leg[off + s], masked.astype(jnp.bfloat16), (((0,), (0,)), ((), ())),
                preferred_element_type=jnp.float32,
            )
            return carry

        lax.fori_loop(0, size, slot, 0, unroll=4)

    def by_row(g, band):
        size = GROUPS[g][1]

        def pair(i, carry):
            first = band * BAND + 2 * i
            rows = [partial[pl.ds(first + j, size, stride=NLW), :] for j in range(2)]
            bands[g][band, pl.ds(pl.multiple_of(i * 2 * size, 2 * size), 2 * size), :] = (
                jnp.concatenate(rows, 0).astype(jnp.bfloat16)
            )
            return carry

        lax.fori_loop(0, BAND // 2, pair, 0, unroll=4)

    def merge(g, band, at, received):
        half = BAND // 2 * GROUPS[g][1]
        step = half // 4

        def part(i, carry):
            rows = pl.ds(pl.multiple_of(at * half + i * step, 32), step)
            other = pl.ds(pl.multiple_of(i * step, 32), step)
            total = bands[g][band, rows, :].astype(jnp.float32) + received[other, :].astype(jnp.float32)
            bands[g][band, rows, :] = total.astype(jnp.bfloat16)
            return carry

        lax.fori_loop(0, 4, part, 0)

    def total(g):
        size = GROUPS[g][1]

        def pair(i, carry):
            rows = pl.ds(pl.multiple_of(i * 2 * size, 2 * size), 2 * size)
            value = bands[g][lat, rows, :].astype(jnp.float32)
            value += sum_dn[g][rows, :].astype(jnp.float32)
            value += sum_up[g][rows, :].astype(jnp.float32)
            mine[g][2 * i] = value[:size].astype(jnp.bfloat16)
            mine[g][2 * i + 1] = value[size:].astype(jnp.bfloat16)
            return carry

        lax.fori_loop(0, BAND // 2, pair, 0, unroll=2)

    def to_row(g, other, sender):
        return pltpu.make_async_remote_copy(
            src_ref=mine[g].at[other], dst_ref=got[g].at[sender],
            send_sem=a_send.at[g, other], recv_sem=a_recv.at[g, sender],
            device_id={"wave": other, "lat": lat}, device_id_type=pl.DeviceIdType.MESH,
        )

    def send_rows(g):
        def one(step, carry):
            to_row(g, peer(step), me).start()
            return carry

        lax.fori_loop(1, N_WAVE, one, 0)
        got[g][me] = mine[g][me]

    def wait_rows(g):
        def one(step, carry):
            to_row(g, me, peer(step)).wait_recv()
            return carry

        lax.fori_loop(1, N_WAVE, one, 0)

    def tables():
        lons = lons_s[row].astype(jnp.float32)
        two = 2.0 * lons
        inverse = 1.0 / jnp.full((8, LANES), two, jnp.float32)

        def spread(r, carry):
            line = waves_v[pl.ds(r, 1), :].astype(jnp.float32)
            m_nat[pl.ds(pl.multiple_of(r * LANES, LANES), LANES), :] = jnp.transpose(
                jnp.broadcast_to(line, (LANES, LANES))
            )
            return carry

        lax.fori_loop(0, M // LANES, spread, 0)

        def regroup(v, carry):
            for off, size in GROUPS:
                m_grp[pl.ds(pl.multiple_of(N_WAVE * off + v * size, 8), size), :] = m_nat[
                    pl.ds(pl.multiple_of(v * SLOTS + off, 8), size), :
                ]
            return carry

        lax.fori_loop(0, N_WAVE, regroup, 0)

        lane = lax.broadcasted_iota(jnp.int32, (8, LANES), 1)
        first = jnp.where(lane < F, LONS - 1.0, 3.0 * LONS - 1.0).astype(jnp.float32)

        def phases(i, carry):
            for j in range(4):
                rows = pl.ds(pl.multiple_of(i * 32 + j * 8, 8), 8)
                m = m_grp[rows, :]
                weight = jnp.where(m == 0.0, 1.0, jnp.where(2.0 * m < lons, 2.0, 0.0))
                c, s = cos_sin(m * first, two, inverse)
                c0[rows, :] = weight * c
                s0[rows, :] = weight * s
                c, s = cos_sin(m * (4.0 * LONS), two, inverse)
                c1[rows, :] = c
                s1[rows, :] = s
            return carry

        lax.fori_loop(0, M // 32, phases, 0)

        for g, (off, size) in enumerate(GROUPS):
            depth = N_WAVE * size

            def columns(i, carry, g=g, off=off, depth=depth):
                base = pl.multiple_of(N_WAVE * off + i * LANES, LANES)
                m = jnp.transpose(m_grp[pl.ds(base, LANES), :])[0:8, :]
                for r in range(0, LONS, 16):
                    parts = []
                    for h in range(2):
                        k = lax.broadcasted_iota(jnp.int32, (8, LANES), 0) + (r + 8 * h)
                        k = (2 * k - (LONS - 1)).astype(jnp.float32)
                        parts.append(cos_sin(m * k, two, inverse))
                    c = jnp.concatenate([p[0] for p in parts], 0)
                    s = jnp.concatenate([p[1] for p in parts], 0)
                    at = pl.multiple_of(i * LANES, LANES)
                    table[g][r : r + 16, pl.ds(at, LANES)] = c.astype(jnp.bfloat16)
                    at = pl.multiple_of(depth + i * LANES, LANES)
                    table[g][r : r + 16, pl.ds(at, LANES)] = (-s).astype(jnp.bfloat16)
                return carry

            lax.fori_loop(0, depth // LANES, columns, 0)

    def rotate(g):
        off, size = GROUPS[g]
        depth = N_WAVE * size

        def pair(i, carry):
            value = jnp.concatenate(
                [got[g][2 * i + j].astype(jnp.float32) for j in range(2)], 0
            )
            swapped = pltpu.roll(value, F, 1)
            lane = lax.broadcasted_iota(jnp.int32, value.shape, 1)
            real = jnp.where(lane < F, value, swapped)
            imag = jnp.where(lane < F, swapped, value)
            rows = pl.ds(pl.multiple_of(N_WAVE * off + i * 2 * size, 16), 2 * size)
            c, s = c0[rows, :], s0[rows, :]
            a, b = real * c - imag * s, real * s + imag * c
            c, s = c1[rows, :], s1[rows, :]
            at = pl.multiple_of(i * 2 * size, 16)
            for p in range(2 * QUADS - 1):
                columns = slice(LANES * (p % 2), LANES * (p % 2) + LANES)
                coef[g][p // 2, pl.ds(at, 2 * size), columns] = a.astype(jnp.bfloat16)
                coef[g][p // 2, pl.ds(depth + at, 2 * size), columns] = b.astype(jnp.bfloat16)
                if p < 2 * QUADS - 2:
                    a, b = a * c - b * s, a * s + b * c
            zero = jnp.zeros((2 * size, LANES), jnp.bfloat16)
            coef[g][QUADS - 1, pl.ds(at, 2 * size), LANES:] = zero
            coef[g][QUADS - 1, pl.ds(depth + at, 2 * size), LANES:] = zero
            return carry

        lax.fori_loop(0, N_WAVE // 2, pair, 0)

    def product(g, quad):
        return jnp.dot(table[g][...], coef[g][quad], preferred_element_type=jnp.float32)

    def to_owner(other, sender):
        return pltpu.make_async_remote_copy(
            src_ref=out.at[other], dst_ref=raw.at[sender],
            send_sem=o_send.at[other], recv_sem=o_recv.at[sender],
            device_id={"wave": other, "lat": lat}, device_id_type=pl.DeviceIdType.MESH,
        )

    def keep():
        return pltpu.make_async_copy(out.at[me], raw.at[me], own_sem)

    limit = most_lons(row)
    last = len(GROUPS) - 1

    copies = [y_copies(g) for g in range(len(GROUPS))]
    legendre_sums(0)
    by_row(0, opp)
    pl.semaphore_wait(barrier, N_WAVE + 1)
    copies[0][0].start()
    copies[0][1].start()
    by_row(0, up)
    copies[0][2].start()
    by_row(0, dn)
    copies[0][3].start()
    by_row(0, lat)
    legendre_sums(1)
    copies[0][0].wait_recv()
    merge(0, up, 0, from_dn[0])
    copies[0][4].start()
    copies[0][1].wait_recv()
    merge(0, dn, 1, from_up[0])
    copies[0][5].start()
    by_row(1, opp)
    copies[1][0].start()
    copies[1][1].start()
    by_row(1, up)
    copies[1][2].start()
    by_row(1, dn)
    copies[1][3].start()
    by_row(1, lat)
    tables()
    copies[1][0].wait_recv()
    merge(1, up, 0, from_dn[1])
    copies[1][4].start()
    copies[1][1].wait_recv()
    merge(1, dn, 1, from_up[1])
    copies[1][5].start()

    for at in range(2, 6):
        copies[0][at].wait_recv()
    total(0)
    send_rows(0)
    for at in range(2, 6):
        copies[1][at].wait_recv()
    total(1)
    send_rows(1)

    wait_rows(0)
    rotate(0)

    def early(quad, carry):
        acc[quad] = product(0, quad)
        return carry

    lax.fori_loop(0, QUADS, early, 0)
    wait_rows(1)
    rotate(1)

    def late(step, carry):
        quad = lax.rem(me // 4 + step, QUADS)
        value = acc[quad] + product(1, quad)
        lane = lax.broadcasted_iota(jnp.int32, (HALF, LANES), 1)
        for p in range(2):
            top = value[:HALF, LANES * p : LANES * (p + 1)]
            bottom = value[HALF:, LANES * p : LANES * (p + 1)]
            even = jnp.where(lane < F, top, pltpu.roll(bottom, F, 1))
            odd = jnp.where(lane < F, pltpu.roll(top, F, 1), bottom)
            out[quad * 4 + 2 * p] = even.astype(jnp.bfloat16)
            out[quad * 4 + 2 * p + 1] = odd.astype(jnp.bfloat16)
        for j in range(4):
            other = quad * 4 + j

            @pl.when((other != me) & (other * LONS < limit))
            def _():
                to_owner(other, me).start()

        return carry

    lax.fori_loop(0, QUADS, late, 0)

    @pl.when(me * LONS < limit)
    def _():
        keep().start()

    def arrived(step, carry):
        sender = peer(step)

        @pl.when(me * LONS < most_lons(lat * BAND + sender))
        def _():
            to_owner(me, sender).wait_recv()

        other = peer(step)

        @pl.when(other * LONS < limit)
        def _():
            to_owner(other, me).wait_send()

        for g in range(len(GROUPS)):
            to_row(g, other, me).wait_send()
        return carry

    lax.fori_loop(1, N_WAVE, arrived, 0)

    @pl.when(me * LONS < limit)
    def _():
        keep().wait()

    for g in range(len(GROUPS)):
        for copy in copies[g]:
            copy.wait_send()


def local(spectra, legendre, wave_list, cycle_lons):
    bf16, f32 = jnp.bfloat16, jnp.float32
    sizes = [size for _, size in GROUPS]
    scratch = [
        pltpu.VMEM((SLOTS, DEPTH, LANES), bf16),
        pltpu.VMEM((SLOTS, DEPTH, LANES), bf16),
        pltpu.VMEM((max(sizes) * NLW, LANES), f32),
    ]
    scratch += [pltpu.VMEM((N_LAT, BAND * n, LANES), bf16) for n in sizes]
    for rows in (BAND // 2, BAND // 2, BAND, BAND):
        scratch += [pltpu.VMEM((rows * n, LANES), bf16) for n in sizes]
    scratch += [pltpu.VMEM((BAND, n, LANES), bf16) for n in sizes]
    scratch += [pltpu.VMEM((N_WAVE, n, LANES), bf16) for n in sizes]
    scratch += [pltpu.VMEM((QUADS, 2 * N_WAVE * n, 2 * LANES), bf16) for n in sizes]
    scratch += [pltpu.VMEM((LONS, 2 * N_WAVE * n), bf16) for n in sizes]
    scratch += [pltpu.VMEM((QUADS, LONS, 2 * LANES), f32), pltpu.VMEM((N_WAVE, HALF, LANES), bf16)]
    scratch += [pltpu.VMEM((M, LANES), f32) for _ in range(6)]
    dma = pltpu.SemaphoreType.DMA
    count = len(GROUPS)
    scratch += [dma((count, 2)), dma((count, 6)), dma((count, 6)), dma((count, N_WAVE))]
    scratch += [dma((count, N_WAVE)), dma((N_WAVE,)), dma((N_WAVE,)), dma]

    raw = pl.pallas_call(
        kernel,
        out_shape=jax.ShapeDtypeStruct((BAND, HALF, LANES), bf16),
        in_specs=[
            pl.BlockSpec(memory_space=pltpu.SMEM),
            pl.BlockSpec(memory_space=pltpu.SMEM),
            pl.BlockSpec(memory_space=pltpu.VMEM),
            pl.BlockSpec(memory_space=pl.ANY),
            pl.BlockSpec(memory_space=pl.ANY),
        ],
        out_specs=pl.BlockSpec(memory_space=pl.ANY),
        scratch_shapes=scratch,
        compiler_params=pltpu.CompilerParams(
            collective_id=0, has_side_effects=True, vmem_limit_bytes=56 * 2**20
        ),
    )(wave_list, cycle_lons, wave_list.reshape(M // LANES, LANES), spectra, legendre)

    first = lax.axis_index("lat") * BAND
    band_lons = lax.dynamic_slice_in_dim(cycle_lons, first, BAND)
    k = lax.axis_index("wave") * LONS + jnp.arange(LONS, dtype=jnp.int32)
    rows = jnp.concatenate([raw[:, :, :F], raw[:, :, F:]], 1)
    return jnp.where((k[None, :] < band_lons[:, None])[:, :, None], rows, jnp.zeros_like(rows))


def solution(mesh):
    in_specs = (P("wave", "lat", None), P("wave", "lat", None), P(), P())
    out_specs = P("lat", "wave", None)
    return jax.shard_map(local, mesh=mesh, in_specs=in_specs, out_specs=out_specs, check_vma=False)
```

```python
import jax
import jax.numpy as jnp
from jax import lax
from jax.experimental import pallas as pl
from jax.experimental.pallas import tpu as pltpu
from jax.sharding import PartitionSpec as P

M = 1280
F = 64
NLW = 128
NLAT = 2560
STRIDE = 20
NLONP = 5632
N_WAVE = 32
N_LAT = 4

SLOTS = M // N_WAVE
DEPTH = M // N_LAT
BAND = NLW // N_LAT
LONS = NLONP // N_WAVE
HALF = LONS // 2
LANES = 128
BLOCK = 2 * LONS
QUADS = N_WAVE // 8
GROUPS = ((0, 24), (24, 16))

COS_TERMS = (
    0.999999009718151, -19.738932854525416, 64.92691787698224,
    -85.24978872544477, 58.68039930519758, -20.879193249375327,
)
SIN_TERMS = (
    6.283184816484557, -41.34156560570182, 81.59907809153451,
    -76.60361308658534, 41.288123420059144, -12.375788874464046,
)


def cos_sin(product, two_lons, inverse):
    turns = jnp.floor(product * inverse + 0.5)
    u = (product - turns * two_lons) * inverse
    z = u * u
    c = jnp.full_like(z, COS_TERMS[-1])
    for term in COS_TERMS[-2::-1]:
        c = c * z + term
    s = jnp.full_like(z, SIN_TERMS[-1])
    for term in SIN_TERMS[-2::-1]:
        s = s * z + term
    return c, s * u


def kernel(waves_s, lons_s, waves_v, spectra, legendre, grid, *scratch):
    names = iter(scratch)
    spec, leg, partial = next(names), next(names), next(names)
    bands, from_dn, from_up, sum_dn, sum_up, mine, got, coef, table = (
        [next(names) for _ in GROUPS] for _ in range(9)
    )
    acc, out, raw, turn, m_nat, m_grp, c0, s0, c1, s1 = (next(names) for _ in range(10))
    in_sem, y_send, y_recv, a_send, a_recv, o_send, o_recv, own_sem, line_sem = names

    me = lax.axis_index("wave")
    lat = lax.axis_index("lat")
    up = lax.rem(lat + 1, N_LAT)
    dn = lax.rem(lat + N_LAT - 1, N_LAT)
    opp = lax.rem(lat + 2, N_LAT)
    row = lat * BAND + me

    def most_lons(w):
        first = STRIDE * w + STRIDE - 1
        last = NLAT - 1 - STRIDE * w
        return 20 + 4 * jnp.minimum(first, last)

    def peer(step):
        return jnp.bitwise_and(me + step, N_WAVE - 1)

    def load(g, which):
        off, size = GROUPS[g]
        source, target = ((spectra, spec), (legendre, leg))[which]
        return pltpu.make_async_copy(
            source.at[pl.ds(off, size)], target.at[pl.ds(off, size)], in_sem.at[g, which]
        )

    for g in range(len(GROUPS)):
        for which in range(2):
            load(g, which).start()

    barrier = pltpu.get_barrier_semaphore()
    for other in (up, dn):
        pl.semaphore_signal(
            barrier, inc=1, device_id={"wave": me, "lat": other}, device_id_type=pl.DeviceIdType.MESH
        )

    def shifted(dx, dz, dcore):
        x = jnp.bitwise_and(me // 8 + dx, 3)
        z = jnp.bitwise_and(me // 2 + dz, 3)
        return x * 8 + z * 2 + jnp.bitwise_xor(jnp.bitwise_and(me, 1), dcore)

    plane = [(dx, 0, dcore) for dx in range(4) for dcore in range(2) if dx or dcore]
    line = [(0, dz, 0) for dz in range(1, 4)]
    for shift in plane + line:
        pl.semaphore_signal(
            barrier, inc=1, device_id={"wave": shifted(*shift), "lat": lat},
            device_id_type=pl.DeviceIdType.MESH,
        )

    def tell():
        for shift in line:
            pl.semaphore_signal(
                line_sem, inc=1, device_id={"wave": shifted(*shift), "lat": lat},
                device_id_type=pl.DeviceIdType.MESH,
            )

    def hear():
        pl.semaphore_wait(line_sem, len(line))

    def along_y(g, at, source, target, other):
        return pltpu.make_async_remote_copy(
            src_ref=source, dst_ref=target, send_sem=y_send.at[g, at], recv_sem=y_recv.at[g, at],
            device_id={"wave": me, "lat": other}, device_id_type=pl.DeviceIdType.MESH,
        )

    def y_copies(g):
        half = BAND // 2 * GROUPS[g][1]
        lo, hi = pl.ds(0, half), pl.ds(half, half)
        b = bands[g]
        return (
            along_y(g, 0, b.at[opp, lo], from_dn[g], up),
            along_y(g, 1, b.at[opp, hi], from_up[g], dn),
            along_y(g, 2, b.at[up, hi], sum_dn[g].at[hi], up),
            along_y(g, 3, b.at[dn, lo], sum_up[g].at[lo], dn),
            along_y(g, 4, b.at[up, lo], sum_dn[g].at[lo], up),
            along_y(g, 5, b.at[dn, hi], sum_up[g].at[hi], dn),
        )

    def legendre_sums(g):
        off, size = GROUPS[g]
        load(g, 0).wait()
        load(g, 1).wait()

        def slot(s, carry):
            live = M - waves_s[me * SLOTS + off + s] - lat * DEPTH
            offsets = lax.broadcasted_iota(jnp.int32, (DEPTH, LANES), 0)
            masked = jnp.where(offsets < live, spec[off + s].astype(jnp.float32), 0.0)
            partial[pl.ds(pl.multiple_of(s * NLW, NLW), NLW), :] = lax.dot_general(
                leg[off + s], masked.astype(jnp.bfloat16), (((0,), (0,)), ((), ())),
                preferred_element_type=jnp.float32,
            )
            return carry

        lax.fori_loop(0, size, slot, 0, unroll=4)

    def by_row(g, band):
        size = GROUPS[g][1]

        def pair(i, carry):
            first = band * BAND + 2 * i
            rows = [partial[pl.ds(first + j, size, stride=NLW), :] for j in range(2)]
            bands[g][band, pl.ds(pl.multiple_of(i * 2 * size, 2 * size), 2 * size), :] = (
                jnp.concatenate(rows, 0).astype(jnp.bfloat16)
            )
            return carry

        lax.fori_loop(0, BAND // 2, pair, 0, unroll=4)

    def merge(g, band, at, received):
        half = BAND // 2 * GROUPS[g][1]
        step = half // 4

        def part(i, carry):
            rows = pl.ds(pl.multiple_of(at * half + i * step, 32), step)
            other = pl.ds(pl.multiple_of(i * step, 32), step)
            total = bands[g][band, rows, :].astype(jnp.float32) + received[other, :].astype(jnp.float32)
            bands[g][band, rows, :] = total.astype(jnp.bfloat16)
            return carry

        lax.fori_loop(0, 4, part, 0)

    def total(g):
        size = GROUPS[g][1]

        def pair(i, carry):
            rows = pl.ds(pl.multiple_of(i * 2 * size, 2 * size), 2 * size)
            value = bands[g][lat, rows, :].astype(jnp.float32)
            value += sum_dn[g][rows, :].astype(jnp.float32)
            value += sum_up[g][rows, :].astype(jnp.float32)
            mine[g][2 * i] = value[:size].astype(jnp.bfloat16)
            mine[g][2 * i + 1] = value[size:].astype(jnp.bfloat16)
            return carry

        lax.fori_loop(0, BAND // 2, pair, 0, unroll=2)

    def to_row(g, other, sender):
        return pltpu.make_async_remote_copy(
            src_ref=mine[g].at[other], dst_ref=got[g].at[sender],
            send_sem=a_send.at[g], recv_sem=a_recv.at[g],
            device_id={"wave": other, "lat": lat}, device_id_type=pl.DeviceIdType.MESH,
        )

    def all_rows(g):
        first = pl.ds(0, N_WAVE - 1)
        return pltpu.make_async_remote_copy(
            src_ref=mine[g].at[first], dst_ref=got[g].at[first],
            send_sem=a_send.at[g], recv_sem=a_recv.at[g],
            device_id={"wave": peer(1), "lat": lat}, device_id_type=pl.DeviceIdType.MESH,
        )

    def send_rows(g):
        for step in range(1, N_WAVE):
            to_row(g, peer(step), me).start()
        got[g][me] = mine[g][me]

    lons = lons_s[row].astype(jnp.float32)
    two = 2.0 * lons

    def reciprocal():
        return 1.0 / jnp.full((8, LANES), two, jnp.float32)

    def phase_tables():
        inverse = reciprocal()

        def spread(r, carry):
            line = waves_v[pl.ds(r, 1), :].astype(jnp.float32)
            m_nat[pl.ds(pl.multiple_of(r * LANES, LANES), LANES), :] = jnp.transpose(
                jnp.broadcast_to(line, (LANES, LANES))
            )
            return carry

        lax.fori_loop(0, M // LANES, spread, 0)

        def regroup(v, carry):
            for off, size in GROUPS:
                m_grp[pl.ds(pl.multiple_of(N_WAVE * off + v * size, 8), size), :] = m_nat[
                    pl.ds(pl.multiple_of(v * SLOTS + off, 8), size), :
                ]
            return carry

        lax.fori_loop(0, N_WAVE, regroup, 0)

        lane = lax.broadcasted_iota(jnp.int32, (8, LANES), 1)
        first = jnp.where(lane < F, BLOCK - 1.0, 3.0 * BLOCK - 1.0).astype(jnp.float32)

        def phases(i, carry):
            for j in range(4):
                rows = pl.ds(pl.multiple_of(i * 32 + j * 8, 8), 8)
                m = m_grp[rows, :]
                weight = jnp.where(m == 0.0, 1.0, jnp.where(2.0 * m < lons, 2.0, 0.0))
                c, s = cos_sin(m * first, two, inverse)
                c0[rows, :] = weight * c
                s0[rows, :] = weight * s
                c, s = cos_sin(m * (4.0 * BLOCK), two, inverse)
                c1[rows, :] = c
                s1[rows, :] = s
            return carry

        lax.fori_loop(0, M // 32, phases, 0)

    def block_tables():
        inverse = reciprocal()
        line = lax.broadcasted_iota(jnp.int32, (8, LANES), 0).astype(jnp.float32)
        for g, (off, size) in enumerate(GROUPS):
            depth = N_WAVE * size

            def columns(i, carry, g=g, off=off, depth=depth):
                base = pl.multiple_of(N_WAVE * off + i * LANES, LANES)
                m = jnp.transpose(m_grp[pl.ds(base, LANES), :])[0:8, :]
                left = pl.ds(pl.multiple_of(i * LANES, LANES), LANES)
                right = pl.ds(pl.multiple_of(depth + i * LANES, LANES), LANES)
                fine = [cos_sin(m * (2.0 * line + 16.0 * h), two, inverse) for h in range(2)]
                fine_c = jnp.concatenate([f[0] for f in fine], 0)
                fine_s = jnp.concatenate([f[1] for f in fine], 0)
                for top in range(0, BLOCK // 16, 8):
                    coarse = m * (32.0 * (line + top) - (BLOCK - 1.0))
                    coarse_c, coarse_s = cos_sin(coarse, two, inverse)
                    for j in range(min(8, BLOCK // 16 - top)):
                        a_c, a_s = coarse_c[j : j + 1], coarse_s[j : j + 1]
                        c = fine_c * a_c - fine_s * a_s
                        s = fine_s * a_c + fine_c * a_s
                        at = 16 * (top + j)
                        table[g][at : at + 16, left] = c.astype(jnp.bfloat16)
                        table[g][at : at + 16, right] = (-s).astype(jnp.bfloat16)
                return carry

            lax.fori_loop(0, depth // LANES, columns, 0)

    def rotate(g):
        off, size = GROUPS[g]
        depth = N_WAVE * size

        def pair(i, carry):
            value = jnp.concatenate(
                [got[g][2 * i + j].astype(jnp.float32) for j in range(2)], 0
            )
            swapped = pltpu.roll(value, F, 1)
            lane = lax.broadcasted_iota(jnp.int32, value.shape, 1)
            real = jnp.where(lane < F, value, swapped)
            imag = jnp.where(lane < F, swapped, value)
            rows = pl.ds(pl.multiple_of(N_WAVE * off + i * 2 * size, 16), 2 * size)
            c, s = c0[rows, :], s0[rows, :]
            a, b = real * c - imag * s, real * s + imag * c
            c, s = c1[rows, :], s1[rows, :]
            at = pl.multiple_of(i * 2 * size, 16)
            for p in range(2 * QUADS):
                columns = slice(LANES * (p % 2), LANES * (p % 2) + LANES)
                coef[g][p // 2, pl.ds(at, 2 * size), columns] = a.astype(jnp.bfloat16)
                coef[g][p // 2, pl.ds(depth + at, 2 * size), columns] = b.astype(jnp.bfloat16)
                if p < 2 * QUADS - 1:
                    a, b = a * c - b * s, a * s + b * c
            return carry

        lax.fori_loop(0, N_WAVE // 2, pair, 0)

    def product(g, quad):
        return jnp.dot(table[g][...], coef[g][quad], preferred_element_type=jnp.float32)

    def to_owner(other, sender):
        return pltpu.make_async_remote_copy(
            src_ref=out.at[other], dst_ref=raw.at[sender],
            send_sem=o_send.at[other], recv_sem=o_recv.at[sender],
            device_id={"wave": other, "lat": lat}, device_id_type=pl.DeviceIdType.MESH,
        )

    limit = most_lons(row)
    last = len(GROUPS) - 1

    copies = [y_copies(g) for g in range(len(GROUPS))]
    legendre_sums(0)
    by_row(0, opp)
    pl.semaphore_wait(barrier, 2 + len(plane) + len(line))
    copies[0][0].start()
    copies[0][1].start()
    tell()
    by_row(0, up)
    by_row(0, dn)
    by_row(0, lat)
    legendre_sums(1)
    by_row(1, opp)
    copies[1][0].start()
    copies[1][1].start()
    copies[0][2].start()
    copies[0][3].start()
    by_row(1, up)
    by_row(1, dn)
    by_row(1, lat)
    phase_tables()
    copies[0][0].wait_recv()
    merge(0, up, 0, from_dn[0])
    copies[0][4].start()
    copies[0][1].wait_recv()
    merge(0, dn, 1, from_up[0])
    copies[0][5].start()
    block_tables()
    copies[1][0].wait_recv()
    merge(1, up, 0, from_dn[1])
    copies[1][1].wait_recv()
    merge(1, dn, 1, from_up[1])
    hear()

    for at in range(2, 6):
        copies[0][at].wait_recv()
    for at in range(2, 6):
        copies[1][at].start()
    total(0)
    send_rows(0)
    for at in range(2, 6):
        copies[1][at].wait_recv()
    total(1)
    send_rows(1)

    all_rows(0).wait_recv()
    rotate(0)

    def early(quad, carry):
        acc[quad] = product(0, quad)
        return carry

    lax.fori_loop(0, QUADS, early, 0)
    all_rows(1).wait_recv()
    rotate(1)

    def late(step, carry):
        quad = jnp.bitwise_and(me // 8 + step, QUADS - 1)
        value = acc[quad] + product(1, quad)
        lane = lax.broadcasted_iota(jnp.int32, (HALF, LANES), 1)
        for p in range(2):
            for c in range(2):
                columns = slice(LANES * p, LANES * (p + 1))
                top = value[LONS * c : LONS * c + HALF, columns]
                bottom = value[LONS * c + HALF : LONS * (c + 1), columns]
                even = jnp.where(lane < F, top, pltpu.roll(bottom, F, 1))
                odd = jnp.where(lane < F, pltpu.roll(top, F, 1), bottom)
                out[quad * 8 + 4 * p + c] = even.astype(jnp.bfloat16)
                out[quad * 8 + 4 * p + 2 + c] = odd.astype(jnp.bfloat16)
        for j in range(8):
            other = quad * 8 + j

            @pl.when((other != me) & (other * LONS < limit))
            def _():
                to_owner(other, me).start()

        return carry

    lax.fori_loop(0, QUADS, late, 0)
    raw[me] = out[me]

    k = me * LONS + lax.broadcasted_iota(jnp.int32, (LONS, F), 0)

    def arrived(step, carry):
        sender = jnp.bitwise_and(me // 8 - step // 8, 3) * 8 + jnp.bitwise_and(me + step, 7)
        w = lat * BAND + sender
        sent = me * LONS < most_lons(w)

        @pl.when(sent & (sender != me))
        def _():
            to_owner(me, sender).wait_recv()

        @pl.when(sent)
        def _():
            halves = raw[sender].astype(jnp.float32)
            lines = jnp.concatenate([halves[:, :F], pltpu.roll(halves, F, 1)[:, :F]], 0)
            turn[sender] = jnp.where(k < lons_s[w], lines, 0.0).astype(jnp.bfloat16)

        @pl.when(jnp.logical_not(sent))
        def _():
            turn[sender] = jnp.zeros((LONS, F), jnp.bfloat16)

        pltpu.make_async_copy(turn.at[sender], grid.at[sender], own_sem).start()
        return carry

    lax.fori_loop(0, N_WAVE, arrived, 0)

    def gone(step, carry):
        other = peer(step)

        @pl.when(other * LONS < limit)
        def _():
            to_owner(other, me).wait_send()

        return carry

    lax.fori_loop(1, N_WAVE, gone, 0)
    for g in range(len(GROUPS)):
        all_rows(g).wait_send()
        for copy in copies[g]:
            copy.wait_send()
    pltpu.make_async_copy(turn, grid, own_sem).wait()


def local(spectra, legendre, wave_list, cycle_lons):
    bf16, f32 = jnp.bfloat16, jnp.float32
    sizes = [size for _, size in GROUPS]
    scratch = [
        pltpu.VMEM((SLOTS, DEPTH, LANES), bf16),
        pltpu.VMEM((SLOTS, DEPTH, LANES), bf16),
        pltpu.VMEM((max(sizes) * NLW, LANES), f32),
    ]
    scratch += [pltpu.VMEM((N_LAT, BAND * n, LANES), bf16) for n in sizes]
    for rows in (BAND // 2, BAND // 2, BAND, BAND):
        scratch += [pltpu.VMEM((rows * n, LANES), bf16) for n in sizes]
    scratch += [pltpu.VMEM((BAND, n, LANES), bf16) for n in sizes]
    scratch += [pltpu.VMEM((N_WAVE, n, LANES), bf16) for n in sizes]
    scratch += [pltpu.VMEM((QUADS, 2 * N_WAVE * n, 2 * LANES), bf16) for n in sizes]
    scratch += [pltpu.VMEM((BLOCK, 2 * N_WAVE * n), bf16) for n in sizes]
    scratch += [pltpu.VMEM((QUADS, BLOCK, 2 * LANES), f32)]
    scratch += [pltpu.VMEM((N_WAVE, HALF, LANES), bf16) for _ in range(2)]
    scratch += [pltpu.VMEM((BAND, LONS, F), bf16)]
    scratch += [pltpu.VMEM((M, LANES), f32) for _ in range(6)]
    dma = pltpu.SemaphoreType.DMA
    count = len(GROUPS)
    scratch += [dma((count, 2)), dma((count, 6)), dma((count, 6)), dma((count,))]
    scratch += [dma((count,)), dma((N_WAVE,)), dma((N_WAVE,)), dma]
    scratch += [pltpu.SemaphoreType.REGULAR]

    return pl.pallas_call(
        kernel,
        out_shape=jax.ShapeDtypeStruct((BAND, LONS, F), bf16),
        in_specs=[
            pl.BlockSpec(memory_space=pltpu.SMEM),
            pl.BlockSpec(memory_space=pltpu.SMEM),
            pl.BlockSpec(memory_space=pltpu.VMEM),
            pl.BlockSpec(memory_space=pl.ANY),
            pl.BlockSpec(memory_space=pl.ANY),
        ],
        out_specs=pl.BlockSpec(memory_space=pl.ANY),
        scratch_shapes=scratch,
        compiler_params=pltpu.CompilerParams(
            collective_id=0, has_side_effects=True, vmem_limit_bytes=56 * 2**20
        ),
    )(wave_list, cycle_lons, wave_list.reshape(M // LANES, LANES), spectra, legendre)


def solution(mesh):
    in_specs = (P("wave", "lat", None), P("wave", "lat", None), P(), P())
    out_specs = P("lat", "wave", None)
    return jax.shard_map(local, mesh=mesh, in_specs=in_specs, out_specs=out_specs, check_vma=False)
```

```python
import jax
import jax.numpy as jnp
from jax import lax
from jax.experimental import pallas as pl
from jax.experimental.pallas import tpu as pltpu
from jax.sharding import PartitionSpec as P

M = 1280
F = 64
NLW = 128
NLAT = 2560
STRIDE = 20
NLONP = 5632
N_WAVE = 32
N_LAT = 4

SLOTS = M // N_WAVE
DEPTH = M // N_LAT
BAND = NLW // N_LAT
LONS = NLONP // N_WAVE
HALF = LONS // 2
LANES = 128
BLOCK = 2 * LONS
QUADS = N_WAVE // 8
GROUPS = ((0, 24), (24, 16))
CHUNK = 8

COS_TERMS = (
    0.999999009718151, -19.738932854525416, 64.92691787698224,
    -85.24978872544477, 58.68039930519758, -20.879193249375327,
)
SIN_TERMS = (
    6.283184816484557, -41.34156560570182, 81.59907809153451,
    -76.60361308658534, 41.288123420059144, -12.375788874464046,
)


def cos_sin(product, two_lons, inverse):
    turns = jnp.floor(product * inverse + 0.5)
    u = (product - turns * two_lons) * inverse
    z = u * u
    c = jnp.full_like(z, COS_TERMS[-1])
    for term in COS_TERMS[-2::-1]:
        c = c * z + term
    s = jnp.full_like(z, SIN_TERMS[-1])
    for term in SIN_TERMS[-2::-1]:
        s = s * z + term
    return c, s * u


def kernel(waves_s, lons_s, waves_v, spectra, legendre, raw, *scratch):
    names = iter(scratch)
    spec, leg, partial = next(names), next(names), next(names)
    bands, from_dn, from_up, sum_dn, sum_up, mine, got, coef, table = (
        [next(names) for _ in GROUPS] for _ in range(9)
    )
    acc, out, m_nat, m_grp, c0, s0, c1, s1 = (next(names) for _ in range(8))
    in_sem, y_send, y_recv, a_send, a_recv, o_send, o_recv, own_sem, line_sem = names

    me = lax.axis_index("wave")
    lat = lax.axis_index("lat")
    up = lax.rem(lat + 1, N_LAT)
    dn = lax.rem(lat + N_LAT - 1, N_LAT)
    opp = lax.rem(lat + 2, N_LAT)
    row = lat * BAND + me

    def most_lons(w):
        first = STRIDE * w + STRIDE - 1
        last = NLAT - 1 - STRIDE * w
        return 20 + 4 * jnp.minimum(first, last)

    def peer(step):
        return jnp.bitwise_and(me + step, N_WAVE - 1)

    def load(chunk, which):
        source, target = ((spectra, spec), (legendre, leg))[which]
        slots = pl.ds(chunk * CHUNK, CHUNK)
        return pltpu.make_async_copy(source.at[slots], target.at[slots], in_sem.at[chunk, which])

    for chunk in range(SLOTS // CHUNK):
        for which in range(2):
            load(chunk, which).start()

    barrier = pltpu.get_barrier_semaphore()
    for other in (up, dn):
        pl.semaphore_signal(
            barrier, inc=1, device_id={"wave": me, "lat": other}, device_id_type=pl.DeviceIdType.MESH
        )

    def shifted(dx, dz, dcore):
        x = jnp.bitwise_and(me // 8 + dx, 3)
        z = jnp.bitwise_and(me // 2 + dz, 3)
        return x * 8 + z * 2 + jnp.bitwise_xor(jnp.bitwise_and(me, 1), dcore)

    plane = [(dx, 0, dcore) for dx in range(4) for dcore in range(2) if dx or dcore]
    line = [(0, dz, 0) for dz in range(1, 4)]
    for shift in plane + line:
        pl.semaphore_signal(
            barrier, inc=1, device_id={"wave": shifted(*shift), "lat": lat},
            device_id_type=pl.DeviceIdType.MESH,
        )

    def tell():
        for shift in line:
            pl.semaphore_signal(
                line_sem, inc=1, device_id={"wave": shifted(*shift), "lat": lat},
                device_id_type=pl.DeviceIdType.MESH,
            )

    def hear():
        pl.semaphore_wait(line_sem, len(line))

    def along_y(g, at, source, target, other):
        return pltpu.make_async_remote_copy(
            src_ref=source, dst_ref=target, send_sem=y_send.at[g, at], recv_sem=y_recv.at[g, at],
            device_id={"wave": me, "lat": other}, device_id_type=pl.DeviceIdType.MESH,
        )

    def y_copies(g):
        half = BAND // 2 * GROUPS[g][1]
        lo, hi = pl.ds(0, half), pl.ds(half, half)
        b = bands[g]
        return (
            along_y(g, 0, b.at[opp, lo], from_dn[g], up),
            along_y(g, 1, b.at[opp, hi], from_up[g], dn),
            along_y(g, 2, b.at[up, hi], sum_dn[g].at[hi], up),
            along_y(g, 3, b.at[dn, lo], sum_up[g].at[lo], dn),
            along_y(g, 4, b.at[up, lo], sum_dn[g].at[lo], up),
            along_y(g, 5, b.at[dn, hi], sum_up[g].at[hi], dn),
        )

    def legendre_sums(g):
        off, size = GROUPS[g]

        def slot(s, carry):
            live = M - waves_s[me * SLOTS + off + s] - lat * DEPTH
            offsets = lax.broadcasted_iota(jnp.int32, (DEPTH, LANES), 0)
            masked = jnp.where(offsets < live, spec[off + s].astype(jnp.float32), 0.0)
            partial[pl.ds(pl.multiple_of(s * NLW, NLW), NLW), :] = lax.dot_general(
                leg[off + s], masked.astype(jnp.bfloat16), (((0,), (0,)), ((), ())),
                preferred_element_type=jnp.float32,
            )
            return carry

        def several(i, carry):
            for which in range(2):
                load(off // CHUNK + i, which).wait()
            return lax.fori_loop(0, CHUNK, lambda j, c: slot(i * CHUNK + j, c), carry, unroll=4)

        lax.fori_loop(0, size // CHUNK, several, 0)

    def by_row(g, band):
        size = GROUPS[g][1]

        def pair(i, carry):
            first = band * BAND + 2 * i
            rows = [partial[pl.ds(first + j, size, stride=NLW), :] for j in range(2)]
            bands[g][band, pl.ds(pl.multiple_of(i * 2 * size, 2 * size), 2 * size), :] = (
                jnp.concatenate(rows, 0).astype(jnp.bfloat16)
            )
            return carry

        lax.fori_loop(0, BAND // 2, pair, 0, unroll=4)

    def merge(g, band, at, received):
        half = BAND // 2 * GROUPS[g][1]
        step = half // 4

        def part(i, carry):
            rows = pl.ds(pl.multiple_of(at * half + i * step, 32), step)
            other = pl.ds(pl.multiple_of(i * step, 32), step)
            total = bands[g][band, rows, :].astype(jnp.float32) + received[other, :].astype(jnp.float32)
            bands[g][band, rows, :] = total.astype(jnp.bfloat16)
            return carry

        lax.fori_loop(0, 4, part, 0)

    def total(g):
        size = GROUPS[g][1]

        def pair(i, carry):
            rows = pl.ds(pl.multiple_of(i * 2 * size, 2 * size), 2 * size)
            value = bands[g][lat, rows, :].astype(jnp.float32)
            value += sum_dn[g][rows, :].astype(jnp.float32)
            value += sum_up[g][rows, :].astype(jnp.float32)
            mine[g][2 * i] = value[:size].astype(jnp.bfloat16)
            mine[g][2 * i + 1] = value[size:].astype(jnp.bfloat16)
            return carry

        lax.fori_loop(0, BAND // 2, pair, 0, unroll=2)

    def to_row(g, other, sender):
        return pltpu.make_async_remote_copy(
            src_ref=mine[g].at[other], dst_ref=got[g].at[sender],
            send_sem=a_send.at[g], recv_sem=a_recv.at[g],
            device_id={"wave": other, "lat": lat}, device_id_type=pl.DeviceIdType.MESH,
        )

    def all_rows(g):
        first = pl.ds(0, N_WAVE - 1)
        return pltpu.make_async_remote_copy(
            src_ref=mine[g].at[first], dst_ref=got[g].at[first],
            send_sem=a_send.at[g], recv_sem=a_recv.at[g],
            device_id={"wave": peer(1), "lat": lat}, device_id_type=pl.DeviceIdType.MESH,
        )

    def send_rows(g):
        for step in range(1, N_WAVE):
            to_row(g, peer(step), me).start()
        got[g][me] = mine[g][me]

    lons = lons_s[row].astype(jnp.float32)
    two = 2.0 * lons

    def reciprocal():
        return 1.0 / jnp.full((8, LANES), two, jnp.float32)

    def phase_tables():
        inverse = reciprocal()

        def spread(r, carry):
            line = waves_v[pl.ds(r, 1), :].astype(jnp.float32)
            m_nat[pl.ds(pl.multiple_of(r * LANES, LANES), LANES), :] = jnp.transpose(
                jnp.broadcast_to(line, (LANES, LANES))
            )
            return carry

        lax.fori_loop(0, M // LANES, spread, 0)

        def regroup(v, carry):
            for off, size in GROUPS:
                m_grp[pl.ds(pl.multiple_of(N_WAVE * off + v * size, 8), size), :] = m_nat[
                    pl.ds(pl.multiple_of(v * SLOTS + off, 8), size), :
                ]
            return carry

        lax.fori_loop(0, N_WAVE, regroup, 0)

        lane = lax.broadcasted_iota(jnp.int32, (8, LANES), 1)
        first = jnp.where(lane < F, BLOCK - 1.0, 3.0 * BLOCK - 1.0).astype(jnp.float32)

        def phases(i, carry):
            for j in range(4):
                rows = pl.ds(pl.multiple_of(i * 32 + j * 8, 8), 8)
                m = m_grp[rows, :]
                weight = jnp.where(m == 0.0, 1.0, jnp.where(2.0 * m < lons, 2.0, 0.0))
                c, s = cos_sin(m * first, two, inverse)
                c0[rows, :] = weight * c
                s0[rows, :] = weight * s
                c, s = cos_sin(m * (4.0 * BLOCK), two, inverse)
                c1[rows, :] = c
                s1[rows, :] = s
            return carry

        lax.fori_loop(0, M // 32, phases, 0)

    def block_tables():
        inverse = reciprocal()
        line = lax.broadcasted_iota(jnp.int32, (8, LANES), 0).astype(jnp.float32)
        for g, (off, size) in enumerate(GROUPS):
            depth = N_WAVE * size

            def columns(i, carry, g=g, off=off, depth=depth):
                base = pl.multiple_of(N_WAVE * off + i * LANES, LANES)
                m = jnp.transpose(m_grp[pl.ds(base, LANES), :])[0:8, :]
                left = pl.ds(pl.multiple_of(i * LANES, LANES), LANES)
                right = pl.ds(pl.multiple_of(depth + i * LANES, LANES), LANES)
                fine = [cos_sin(m * (2.0 * line + 16.0 * h), two, inverse) for h in range(2)]
                fine_c = jnp.concatenate([f[0] for f in fine], 0)
                fine_s = jnp.concatenate([f[1] for f in fine], 0)
                for top in range(0, BLOCK // 16, 8):
                    coarse = m * (32.0 * (line + top) - (BLOCK - 1.0))
                    coarse_c, coarse_s = cos_sin(coarse, two, inverse)
                    for j in range(min(8, BLOCK // 16 - top)):
                        a_c, a_s = coarse_c[j : j + 1], coarse_s[j : j + 1]
                        c = fine_c * a_c - fine_s * a_s
                        s = fine_s * a_c + fine_c * a_s
                        at = 16 * (top + j)
                        table[g][at : at + 16, left] = c.astype(jnp.bfloat16)
                        table[g][at : at + 16, right] = (-s).astype(jnp.bfloat16)
                return carry

            lax.fori_loop(0, depth // LANES, columns, 0)

    def rotate(g):
        off, size = GROUPS[g]
        depth = N_WAVE * size

        def pair(i, carry):
            value = jnp.concatenate(
                [got[g][2 * i + j].astype(jnp.float32) for j in range(2)], 0
            )
            swapped = pltpu.roll(value, F, 1)
            lane = lax.broadcasted_iota(jnp.int32, value.shape, 1)
            real = jnp.where(lane < F, value, swapped)
            imag = jnp.where(lane < F, swapped, value)
            rows = pl.ds(pl.multiple_of(N_WAVE * off + i * 2 * size, 16), 2 * size)
            c, s = c0[rows, :], s0[rows, :]
            a, b = real * c - imag * s, real * s + imag * c
            c, s = c1[rows, :], s1[rows, :]
            at = pl.multiple_of(i * 2 * size, 16)
            for p in range(2 * QUADS):
                columns = slice(LANES * (p % 2), LANES * (p % 2) + LANES)
                coef[g][p // 2, pl.ds(at, 2 * size), columns] = a.astype(jnp.bfloat16)
                coef[g][p // 2, pl.ds(depth + at, 2 * size), columns] = b.astype(jnp.bfloat16)
                if p < 2 * QUADS - 1:
                    a, b = a * c - b * s, a * s + b * c
            return carry

        lax.fori_loop(0, N_WAVE // 2, pair, 0)

    def product(g, quad):
        return jnp.dot(table[g][...], coef[g][quad], preferred_element_type=jnp.float32)

    def to_owner(other, sender):
        return pltpu.make_async_remote_copy(
            src_ref=out.at[other], dst_ref=raw.at[sender],
            send_sem=o_send.at[other], recv_sem=o_recv.at[sender],
            device_id={"wave": other, "lat": lat}, device_id_type=pl.DeviceIdType.MESH,
        )

    def far_first(step):
        return jnp.where(step == 0, 2, jnp.where(step == 1, 1, jnp.where(step == 2, 3, 0)))

    limit = most_lons(row)
    last = len(GROUPS) - 1

    copies = [y_copies(g) for g in range(len(GROUPS))]
    legendre_sums(0)
    by_row(0, opp)
    pl.semaphore_wait(barrier, 2 + len(plane) + len(line))
    copies[0][0].start()
    copies[0][1].start()
    tell()
    by_row(0, up)
    by_row(0, dn)
    by_row(0, lat)
    legendre_sums(1)
    by_row(1, opp)
    copies[1][0].start()
    copies[1][1].start()
    copies[0][2].start()
    copies[0][3].start()
    by_row(1, up)
    by_row(1, dn)
    by_row(1, lat)
    phase_tables()
    copies[0][0].wait_recv()
    merge(0, up, 0, from_dn[0])
    copies[0][4].start()
    copies[0][1].wait_recv()
    merge(0, dn, 1, from_up[0])
    copies[0][5].start()
    block_tables()
    copies[1][0].wait_recv()
    merge(1, up, 0, from_dn[1])
    copies[1][1].wait_recv()
    merge(1, dn, 1, from_up[1])
    hear()

    for at in range(2, 6):
        copies[0][at].wait_recv()
    for at in range(2, 6):
        copies[1][at].start()
    total(0)
    send_rows(0)
    for at in range(2, 6):
        copies[1][at].wait_recv()
    total(1)
    send_rows(1)

    all_rows(0).wait_recv()
    rotate(0)

    def early(quad, carry):
        acc[quad] = product(0, quad)
        return carry

    lax.fori_loop(0, QUADS, early, 0)
    all_rows(1).wait_recv()
    rotate(1)

    def late(step, carry):
        quad = jnp.bitwise_and(me // 8 + far_first(step), QUADS - 1)
        value = acc[quad] + product(1, quad)
        lane = lax.broadcasted_iota(jnp.int32, (HALF, LANES), 1)
        for p in range(2):
            for c in range(2):
                columns = slice(LANES * p, LANES * (p + 1))
                top = value[LONS * c : LONS * c + HALF, columns]
                bottom = value[LONS * c + HALF : LONS * (c + 1), columns]
                even = jnp.where(lane < F, top, pltpu.roll(bottom, F, 1))
                odd = jnp.where(lane < F, pltpu.roll(top, F, 1), bottom)
                out[quad * 8 + 4 * p + c] = even.astype(jnp.bfloat16)
                out[quad * 8 + 4 * p + 2 + c] = odd.astype(jnp.bfloat16)
        for j in range(8):
            other = quad * 8 + j

            @pl.when((other != me) & (other * LONS < limit))
            def _():
                to_owner(other, me).start()

        return carry

    lax.fori_loop(0, QUADS, late, 0)
    keep = pltpu.make_async_copy(out.at[me], raw.at[me], own_sem)
    keep.start()

    def arrived(step, carry):
        sender = jnp.bitwise_and(me // 8 - far_first(step // 8), 3) * 8 + jnp.bitwise_and(me + step, 7)

        @pl.when((me * LONS < most_lons(lat * BAND + sender)) & (sender != me))
        def _():
            to_owner(me, sender).wait_recv()

        return carry

    lax.fori_loop(0, N_WAVE, arrived, 0)

    def gone(step, carry):
        other = peer(step)

        @pl.when(other * LONS < limit)
        def _():
            to_owner(other, me).wait_send()

        return carry

    lax.fori_loop(1, N_WAVE, gone, 0)
    for g in range(len(GROUPS)):
        all_rows(g).wait_send()
        for copy in copies[g]:
            copy.wait_send()
    keep.wait()


def unpack_kernel(lons_s, raw, grid):
    first = lax.axis_index("lat") * BAND
    k = lax.axis_index("wave") * LONS + lax.broadcasted_iota(jnp.int32, (F, LONS), 1)
    for w in range(BAND):
        turned = jnp.transpose(raw[w]).astype(jnp.float32)
        line = jnp.concatenate([turned[:F], turned[F:]], 1)
        grid[w] = jnp.where(k < lons_s[first + w], line, 0.0).astype(jnp.bfloat16)


def local(spectra, legendre, wave_list, cycle_lons):
    bf16, f32 = jnp.bfloat16, jnp.float32
    sizes = [size for _, size in GROUPS]
    scratch = [
        pltpu.VMEM((SLOTS, DEPTH, LANES), bf16),
        pltpu.VMEM((SLOTS, DEPTH, LANES), bf16),
        pltpu.VMEM((max(sizes) * NLW, LANES), f32),
    ]
    scratch += [pltpu.VMEM((N_LAT, BAND * n, LANES), bf16) for n in sizes]
    for rows in (BAND // 2, BAND // 2, BAND, BAND):
        scratch += [pltpu.VMEM((rows * n, LANES), bf16) for n in sizes]
    scratch += [pltpu.VMEM((BAND, n, LANES), bf16) for n in sizes]
    scratch += [pltpu.VMEM((N_WAVE, n, LANES), bf16) for n in sizes]
    scratch += [pltpu.VMEM((QUADS, 2 * N_WAVE * n, 2 * LANES), bf16) for n in sizes]
    scratch += [pltpu.VMEM((BLOCK, 2 * N_WAVE * n), bf16) for n in sizes]
    scratch += [pltpu.VMEM((QUADS, BLOCK, 2 * LANES), f32)]
    scratch += [pltpu.VMEM((N_WAVE, HALF, LANES), bf16)]
    scratch += [pltpu.VMEM((M, LANES), f32) for _ in range(6)]
    dma = pltpu.SemaphoreType.DMA
    count = len(GROUPS)
    scratch += [dma((SLOTS // CHUNK, 2)), dma((count, 6)), dma((count, 6)), dma((count,))]
    scratch += [dma((count,)), dma((N_WAVE,)), dma((N_WAVE,)), dma]
    scratch += [pltpu.SemaphoreType.REGULAR]

    raw = pl.pallas_call(
        kernel,
        out_shape=jax.ShapeDtypeStruct((BAND, HALF, LANES), bf16),
        in_specs=[
            pl.BlockSpec(memory_space=pltpu.SMEM),
            pl.BlockSpec(memory_space=pltpu.SMEM),
            pl.BlockSpec(memory_space=pltpu.VMEM),
            pl.BlockSpec(memory_space=pl.ANY),
            pl.BlockSpec(memory_space=pl.ANY),
        ],
        out_specs=pl.BlockSpec(memory_space=pl.ANY),
        scratch_shapes=scratch,
        compiler_params=pltpu.CompilerParams(
            collective_id=0, has_side_effects=True, vmem_limit_bytes=56 * 2**20
        ),
    )(wave_list, cycle_lons, wave_list.reshape(M // LANES, LANES), spectra, legendre)
    grid = pl.pallas_call(
        unpack_kernel,
        out_shape=jax.ShapeDtypeStruct((BAND, F, LONS), bf16),
        in_specs=[pl.BlockSpec(memory_space=pltpu.SMEM), pl.BlockSpec(memory_space=pltpu.VMEM)],
        out_specs=pl.BlockSpec(memory_space=pltpu.VMEM),
    )(cycle_lons, raw)
    return jnp.transpose(grid, (0, 2, 1))


def solution(mesh):
    in_specs = (P("wave", "lat", None), P("wave", "lat", None), P(), P())
    out_specs = P("lat", "wave", None)
    return jax.shard_map(local, mesh=mesh, in_specs=in_specs, out_specs=out_specs, check_vma=False)
```

```python
import jax
import jax.numpy as jnp
from jax import lax
from jax.experimental import pallas as pl
from jax.experimental.pallas import tpu as pltpu
from jax.sharding import PartitionSpec as P

M = 1280
F = 64
NLW = 128
NLAT = 2560
STRIDE = 20
NLONP = 5632
N_WAVE = 32
N_LAT = 4

SLOTS = M // N_WAVE
DEPTH = M // N_LAT
BAND = NLW // N_LAT
LONS = NLONP // N_WAVE
HALF = LONS // 2
LANES = 128
BLOCK = 2 * LONS
QUADS = N_WAVE // 8
GROUPS = ((0, 16), (16, 24))
CHUNK = 8
FAR_FIRST = sorted(
    [(x, z, c) for x in range(4) for z in range(4) for c in range(2) if x or z or c],
    key=lambda s: (-min(s[0], 4 - s[0]) - min(s[1], 4 - s[1]), s),
)

COS_TERMS = (
    0.999999009718151, -19.738932854525416, 64.92691787698224,
    -85.24978872544477, 58.68039930519758, -20.879193249375327,
)
SIN_TERMS = (
    6.283184816484557, -41.34156560570182, 81.59907809153451,
    -76.60361308658534, 41.288123420059144, -12.375788874464046,
)


def cos_sin(product, two_lons, inverse):
    turns = jnp.floor(product * inverse + 0.5)
    u = (product - turns * two_lons) * inverse
    z = u * u
    c = jnp.full_like(z, COS_TERMS[-1])
    for term in COS_TERMS[-2::-1]:
        c = c * z + term
    s = jnp.full_like(z, SIN_TERMS[-1])
    for term in SIN_TERMS[-2::-1]:
        s = s * z + term
    return c, s * u


def kernel(waves_s, lons_s, waves_v, spectra, legendre, raw, *scratch):
    names = iter(scratch)
    spec, leg, partial = next(names), next(names), next(names)
    bands, from_dn, from_up, sum_dn, sum_up, mine, got, coef, table = (
        [next(names) for _ in GROUPS] for _ in range(9)
    )
    acc, out, m_nat, m_grp, c0, s0, c1, s1 = (next(names) for _ in range(8))
    in_sem, y_send, y_recv, a_send, a_recv, o_send, o_recv, own_sem, line_sem = names

    me = lax.axis_index("wave")
    lat = lax.axis_index("lat")
    up = lax.rem(lat + 1, N_LAT)
    dn = lax.rem(lat + N_LAT - 1, N_LAT)
    opp = lax.rem(lat + 2, N_LAT)
    row = lat * BAND + me

    def most_lons(w):
        first = STRIDE * w + STRIDE - 1
        last = NLAT - 1 - STRIDE * w
        return 20 + 4 * jnp.minimum(first, last)

    def peer(step):
        return jnp.bitwise_and(me + step, N_WAVE - 1)

    def load(chunk, which):
        source, target = ((spectra, spec), (legendre, leg))[which]
        slots = pl.ds(chunk * CHUNK, CHUNK)
        return pltpu.make_async_copy(source.at[slots], target.at[slots], in_sem.at[chunk, which])

    for chunk in range(SLOTS // CHUNK):
        for which in range(2):
            load(chunk, which).start()

    barrier = pltpu.get_barrier_semaphore()
    for other in (up, dn):
        pl.semaphore_signal(
            barrier, inc=1, device_id={"wave": me, "lat": other}, device_id_type=pl.DeviceIdType.MESH
        )

    def shifted(dx, dz, dcore):
        x = jnp.bitwise_and(me // 8 + dx, 3)
        z = jnp.bitwise_and(me // 2 + dz, 3)
        return x * 8 + z * 2 + jnp.bitwise_xor(jnp.bitwise_and(me, 1), dcore)

    plane = [(dx, 0, dcore) for dx in range(4) for dcore in range(2) if dx or dcore]
    line = [(0, dz, 0) for dz in range(1, 4)]
    for shift in plane + line:
        pl.semaphore_signal(
            barrier, inc=1, device_id={"wave": shifted(*shift), "lat": lat},
            device_id_type=pl.DeviceIdType.MESH,
        )

    def tell():
        for shift in line:
            pl.semaphore_signal(
                line_sem, inc=1, device_id={"wave": shifted(*shift), "lat": lat},
                device_id_type=pl.DeviceIdType.MESH,
            )

    def hear():
        pl.semaphore_wait(line_sem, len(line))

    def along_y(g, at, source, target, other):
        return pltpu.make_async_remote_copy(
            src_ref=source, dst_ref=target, send_sem=y_send.at[g, at], recv_sem=y_recv.at[g, at],
            device_id={"wave": me, "lat": other}, device_id_type=pl.DeviceIdType.MESH,
        )

    def y_copies(g):
        half = BAND // 2 * GROUPS[g][1]
        lo, hi = pl.ds(0, half), pl.ds(half, half)
        b = bands[g]
        return (
            along_y(g, 0, b.at[opp, lo], from_dn[g], up),
            along_y(g, 1, b.at[opp, hi], from_up[g], dn),
            along_y(g, 2, b.at[up, hi], sum_dn[g].at[hi], up),
            along_y(g, 3, b.at[dn, lo], sum_up[g].at[lo], dn),
            along_y(g, 4, b.at[up, lo], sum_dn[g].at[lo], up),
            along_y(g, 5, b.at[dn, hi], sum_up[g].at[hi], dn),
        )

    def legendre_sums(g):
        off, size = GROUPS[g]

        def slot(s, carry):
            live = M - waves_s[me * SLOTS + off + s] - lat * DEPTH
            offsets = lax.broadcasted_iota(jnp.int32, (DEPTH, LANES), 0)
            masked = jnp.where(offsets < live, spec[off + s].astype(jnp.float32), 0.0)
            partial[pl.ds(pl.multiple_of(s * NLW, NLW), NLW), :] = lax.dot_general(
                leg[off + s], masked.astype(jnp.bfloat16), (((0,), (0,)), ((), ())),
                preferred_element_type=jnp.float32,
            )
            return carry

        def several(i, carry):
            for which in range(2):
                load(off // CHUNK + i, which).wait()
            return lax.fori_loop(0, CHUNK, lambda j, c: slot(i * CHUNK + j, c), carry, unroll=8)

        lax.fori_loop(0, size // CHUNK, several, 0)

    def by_row(g, band):
        size = GROUPS[g][1]

        def pair(i, carry):
            first = band * BAND + 2 * i
            rows = [partial[pl.ds(first + j, size, stride=NLW), :] for j in range(2)]
            bands[g][band, pl.ds(pl.multiple_of(i * 2 * size, 2 * size), 2 * size), :] = (
                jnp.concatenate(rows, 0).astype(jnp.bfloat16)
            )
            return carry

        lax.fori_loop(0, BAND // 2, pair, 0, unroll=16)

    def merge(g, band, at, received):
        half = BAND // 2 * GROUPS[g][1]
        step = half // 4

        def part(i, carry):
            rows = pl.ds(pl.multiple_of(at * half + i * step, 32), step)
            other = pl.ds(pl.multiple_of(i * step, 32), step)
            total = bands[g][band, rows, :].astype(jnp.float32) + received[other, :].astype(jnp.float32)
            bands[g][band, rows, :] = total.astype(jnp.bfloat16)
            return carry

        lax.fori_loop(0, 4, part, 0, unroll=4)

    def total(g):
        size = GROUPS[g][1]

        def pair(i, carry):
            rows = pl.ds(pl.multiple_of(i * 2 * size, 2 * size), 2 * size)
            value = bands[g][lat, rows, :].astype(jnp.float32)
            value += sum_dn[g][rows, :].astype(jnp.float32)
            value += sum_up[g][rows, :].astype(jnp.float32)
            mine[g][2 * i] = value[:size].astype(jnp.bfloat16)
            mine[g][2 * i + 1] = value[size:].astype(jnp.bfloat16)
            return carry

        lax.fori_loop(0, BAND // 2, pair, 0, unroll=8)

    def to_row(g, other, sender):
        return pltpu.make_async_remote_copy(
            src_ref=mine[g].at[other], dst_ref=got[g].at[sender],
            send_sem=a_send.at[g], recv_sem=a_recv.at[g],
            device_id={"wave": other, "lat": lat}, device_id_type=pl.DeviceIdType.MESH,
        )

    def all_rows(g):
        first = pl.ds(0, N_WAVE - 1)
        return pltpu.make_async_remote_copy(
            src_ref=mine[g].at[first], dst_ref=got[g].at[first],
            send_sem=a_send.at[g], recv_sem=a_recv.at[g],
            device_id={"wave": peer(1), "lat": lat}, device_id_type=pl.DeviceIdType.MESH,
        )

    def send_rows(g):
        for shift in FAR_FIRST:
            to_row(g, shifted(*shift), me).start()
        got[g][me] = mine[g][me]

    lons = lons_s[row].astype(jnp.float32)
    two = 2.0 * lons

    def reciprocal():
        return 1.0 / jnp.full((8, LANES), two, jnp.float32)

    def phase_tables():
        inverse = reciprocal()

        def spread(r, carry):
            line = waves_v[pl.ds(r, 1), :].astype(jnp.float32)
            m_nat[pl.ds(pl.multiple_of(r * LANES, LANES), LANES), :] = jnp.transpose(
                jnp.broadcast_to(line, (LANES, LANES))
            )
            return carry

        lax.fori_loop(0, M // LANES, spread, 0, unroll=5)

        def regroup(v, carry):
            for off, size in GROUPS:
                m_grp[pl.ds(pl.multiple_of(N_WAVE * off + v * size, 8), size), :] = m_nat[
                    pl.ds(pl.multiple_of(v * SLOTS + off, 8), size), :
                ]
            return carry

        lax.fori_loop(0, N_WAVE, regroup, 0, unroll=4)

        lane = lax.broadcasted_iota(jnp.int32, (8, LANES), 1)
        first = jnp.where(lane < F, BLOCK - 1.0, 3.0 * BLOCK - 1.0).astype(jnp.float32)

        def phases(i, carry):
            for j in range(4):
                rows = pl.ds(pl.multiple_of(i * 32 + j * 8, 8), 8)
                m = m_grp[rows, :]
                weight = jnp.where(m == 0.0, 1.0, jnp.where(2.0 * m < lons, 2.0, 0.0))
                c, s = cos_sin(m * first, two, inverse)
                c0[rows, :] = weight * c
                s0[rows, :] = weight * s
                c, s = cos_sin(m * (4.0 * BLOCK), two, inverse)
                c1[rows, :] = c
                s1[rows, :] = s
            return carry

        lax.fori_loop(0, M // 32, phases, 0, unroll=2)

    def block_tables():
        inverse = reciprocal()
        line = lax.broadcasted_iota(jnp.int32, (8, LANES), 0).astype(jnp.float32)
        for g, (off, size) in enumerate(GROUPS):
            depth = N_WAVE * size

            def columns(i, carry, g=g, off=off, depth=depth):
                base = pl.multiple_of(N_WAVE * off + i * LANES, LANES)
                m = jnp.transpose(m_grp[pl.ds(base, LANES), :])[0:8, :]
                left = pl.ds(pl.multiple_of(i * LANES, LANES), LANES)
                right = pl.ds(pl.multiple_of(depth + i * LANES, LANES), LANES)
                fine = [cos_sin(m * (2.0 * line + 16.0 * h), two, inverse) for h in range(2)]
                fine_c = jnp.concatenate([f[0] for f in fine], 0)
                fine_s = jnp.concatenate([f[1] for f in fine], 0)
                for top in range(0, BLOCK // 16, 8):
                    coarse = m * (32.0 * (line + top) - (BLOCK - 1.0))
                    coarse_c, coarse_s = cos_sin(coarse, two, inverse)
                    for j in range(min(8, BLOCK // 16 - top)):
                        a_c, a_s = coarse_c[j : j + 1], coarse_s[j : j + 1]
                        c = fine_c * a_c - fine_s * a_s
                        s = fine_s * a_c + fine_c * a_s
                        at = 16 * (top + j)
                        table[g][at : at + 16, left] = c.astype(jnp.bfloat16)
                        table[g][at : at + 16, right] = (-s).astype(jnp.bfloat16)
                return carry

            lax.fori_loop(0, depth // LANES, columns, 0)

    def rotate(g):
        off, size = GROUPS[g]
        depth = N_WAVE * size

        def pair(i, carry):
            value = jnp.concatenate(
                [got[g][2 * i + j].astype(jnp.float32) for j in range(2)], 0
            )
            swapped = pltpu.roll(value, F, 1)
            lane = lax.broadcasted_iota(jnp.int32, value.shape, 1)
            real = jnp.where(lane < F, value, swapped)
            imag = jnp.where(lane < F, swapped, value)
            rows = pl.ds(pl.multiple_of(N_WAVE * off + i * 2 * size, 16), 2 * size)
            c, s = c0[rows, :], s0[rows, :]
            a, b = real * c - imag * s, real * s + imag * c
            c, s = c1[rows, :], s1[rows, :]
            at = pl.multiple_of(i * 2 * size, 16)
            for p in range(2 * QUADS):
                columns = slice(LANES * (p % 2), LANES * (p % 2) + LANES)
                coef[g][p // 2, pl.ds(at, 2 * size), columns] = a.astype(jnp.bfloat16)
                coef[g][p // 2, pl.ds(depth + at, 2 * size), columns] = b.astype(jnp.bfloat16)
                if p < 2 * QUADS - 1:
                    a, b = a * c - b * s, a * s + b * c
            return carry

        lax.fori_loop(0, N_WAVE // 2, pair, 0, unroll=4)

    def product(g, quad):
        return jnp.dot(table[g][...], coef[g][quad], preferred_element_type=jnp.float32)

    def to_owner(other, sender):
        return pltpu.make_async_remote_copy(
            src_ref=out.at[other], dst_ref=raw.at[sender],
            send_sem=o_send.at[other], recv_sem=o_recv.at[sender],
            device_id={"wave": other, "lat": lat}, device_id_type=pl.DeviceIdType.MESH,
        )

    def far_first(step):
        return jnp.where(step == 0, 2, jnp.where(step == 1, 3, jnp.where(step == 2, 1, 0)))

    limit = most_lons(row)
    last = len(GROUPS) - 1

    copies = [y_copies(g) for g in range(len(GROUPS))]
    legendre_sums(0)
    by_row(0, opp)
    pl.semaphore_wait(barrier, 2 + len(plane) + len(line))
    copies[0][0].start()
    copies[0][1].start()
    tell()
    by_row(0, up)
    by_row(0, dn)
    by_row(0, lat)
    legendre_sums(1)
    by_row(1, opp)
    copies[1][0].start()
    copies[1][1].start()
    copies[0][2].start()
    copies[0][3].start()
    by_row(1, up)
    by_row(1, dn)
    by_row(1, lat)
    phase_tables()
    copies[0][0].wait_recv()
    merge(0, up, 0, from_dn[0])
    copies[0][4].start()
    copies[0][1].wait_recv()
    merge(0, dn, 1, from_up[0])
    copies[0][5].start()
    block_tables()
    copies[1][0].wait_recv()
    merge(1, up, 0, from_dn[1])
    copies[1][1].wait_recv()
    merge(1, dn, 1, from_up[1])
    for at in range(2, 6):
        copies[1][at].start()
    hear()

    for at in range(2, 6):
        copies[0][at].wait_recv()
    total(0)
    send_rows(0)
    for at in range(2, 6):
        copies[1][at].wait_recv()
    total(1)
    send_rows(1)

    all_rows(0).wait_recv()
    rotate(0)

    def early(quad, carry):
        acc[quad] = product(0, quad)
        return carry

    lax.fori_loop(0, QUADS, early, 0)
    all_rows(1).wait_recv()
    rotate(1)

    def late(step, carry):
        quad = jnp.bitwise_and(me // 8 + far_first(step), QUADS - 1)
        value = acc[quad] + product(1, quad)
        lane = lax.broadcasted_iota(jnp.int32, (HALF, LANES), 1)
        for p in range(2):
            for c in range(2):
                columns = slice(LANES * p, LANES * (p + 1))
                top = value[LONS * c : LONS * c + HALF, columns]
                bottom = value[LONS * c + HALF : LONS * (c + 1), columns]
                even = jnp.where(lane < F, top, pltpu.roll(bottom, F, 1))
                odd = jnp.where(lane < F, pltpu.roll(top, F, 1), bottom)
                out[quad * 8 + 4 * p + c] = even.astype(jnp.bfloat16)
                out[quad * 8 + 4 * p + 2 + c] = odd.astype(jnp.bfloat16)
        for j in range(8):
            other = quad * 8 + j

            @pl.when((other != me) & (other * LONS < limit))
            def _():
                to_owner(other, me).start()

        return carry

    lax.fori_loop(0, QUADS, late, 0)
    keep = pltpu.make_async_copy(out.at[me], raw.at[me], own_sem)
    keep.start()

    def gone(step, carry):
        other = peer(step)

        @pl.when(other * LONS < limit)
        def _():
            to_owner(other, me).wait_send()

        return carry

    lax.fori_loop(1, N_WAVE, gone, 0)
    for g in range(len(GROUPS)):
        all_rows(g).wait_send()
        for copy in copies[g]:
            copy.wait_send()
    def arrived(step, carry):
        sender = jnp.bitwise_and(me // 8 - far_first(step // 8), 3) * 8 + jnp.bitwise_and(me + step, 7)

        @pl.when((me * LONS < most_lons(lat * BAND + sender)) & (sender != me))
        def _():
            to_owner(me, sender).wait_recv()

        return carry

    lax.fori_loop(0, N_WAVE, arrived, 0)
    keep.wait()


def unpack_kernel(lons_s, raw, grid):
    first = lax.axis_index("lat") * BAND
    k = lax.axis_index("wave") * LONS + lax.broadcasted_iota(jnp.int32, (F, LONS), 1)
    for w in range(BAND):
        turned = jnp.transpose(raw[w]).astype(jnp.float32)
        line = jnp.concatenate([turned[:F], turned[F:]], 1)
        grid[w] = jnp.where(k < lons_s[first + w], line, 0.0).astype(jnp.bfloat16)


def local(spectra, legendre, wave_list, cycle_lons):
    bf16, f32 = jnp.bfloat16, jnp.float32
    sizes = [size for _, size in GROUPS]
    scratch = [
        pltpu.VMEM((SLOTS, DEPTH, LANES), bf16),
        pltpu.VMEM((SLOTS, DEPTH, LANES), bf16),
        pltpu.VMEM((max(sizes) * NLW, LANES), f32),
    ]
    scratch += [pltpu.VMEM((N_LAT, BAND * n, LANES), bf16) for n in sizes]
    for rows in (BAND // 2, BAND // 2, BAND, BAND):
        scratch += [pltpu.VMEM((rows * n, LANES), bf16) for n in sizes]
    scratch += [pltpu.VMEM((BAND, n, LANES), bf16) for n in sizes]
    scratch += [pltpu.VMEM((N_WAVE, n, LANES), bf16) for n in sizes]
    scratch += [pltpu.VMEM((QUADS, 2 * N_WAVE * n, 2 * LANES), bf16) for n in sizes]
    scratch += [pltpu.VMEM((BLOCK, 2 * N_WAVE * n), bf16) for n in sizes]
    scratch += [pltpu.VMEM((QUADS, BLOCK, 2 * LANES), f32)]
    scratch += [pltpu.VMEM((N_WAVE, HALF, LANES), bf16)]
    scratch += [pltpu.VMEM((M, LANES), f32) for _ in range(6)]
    dma = pltpu.SemaphoreType.DMA
    count = len(GROUPS)
    scratch += [dma((SLOTS // CHUNK, 2)), dma((count, 6)), dma((count, 6)), dma((count,))]
    scratch += [dma((count,)), dma((N_WAVE,)), dma((N_WAVE,)), dma]
    scratch += [pltpu.SemaphoreType.REGULAR]

    raw = pl.pallas_call(
        kernel,
        out_shape=jax.ShapeDtypeStruct((BAND, HALF, LANES), bf16),
        in_specs=[
            pl.BlockSpec(memory_space=pltpu.SMEM),
            pl.BlockSpec(memory_space=pltpu.SMEM),
            pl.BlockSpec(memory_space=pltpu.VMEM),
            pl.BlockSpec(memory_space=pl.ANY),
            pl.BlockSpec(memory_space=pl.ANY),
        ],
        out_specs=pl.BlockSpec(memory_space=pl.ANY),
        scratch_shapes=scratch,
        compiler_params=pltpu.CompilerParams(
            collective_id=0, has_side_effects=True, vmem_limit_bytes=56 * 2**20
        ),
    )(wave_list, cycle_lons, wave_list.reshape(M // LANES, LANES), spectra, legendre)
    grid = pl.pallas_call(
        unpack_kernel,
        out_shape=jax.ShapeDtypeStruct((BAND, F, LONS), bf16),
        in_specs=[pl.BlockSpec(memory_space=pltpu.SMEM), pl.BlockSpec(memory_space=pltpu.VMEM)],
        out_specs=pl.BlockSpec(memory_space=pltpu.VMEM),
    )(cycle_lons, raw)
    return jnp.transpose(grid, (0, 2, 1))


def solution(mesh):
    in_specs = (P("wave", "lat", None), P("wave", "lat", None), P(), P())
    out_specs = P("lat", "wave", None)
    return jax.shard_map(local, mesh=mesh, in_specs=in_specs, out_specs=out_specs, check_vma=False)
```

```python
import jax
import jax.numpy as jnp
from jax import lax
from jax.experimental import pallas as pl
from jax.experimental.pallas import tpu as pltpu
from jax.sharding import PartitionSpec as P

M = 1280
F = 64
NLW = 128
NLAT = 2560
STRIDE = 20
NLONP = 5632
N_WAVE = 32
N_LAT = 4

SLOTS = M // N_WAVE
DEPTH = M // N_LAT
BAND = NLW // N_LAT
LONS = NLONP // N_WAVE
HALF = LONS // 2
LANES = 128
BLOCK = 2 * LONS
QUADS = N_WAVE // 8
GROUPS = ((0, 16), (16, 24))
CHUNK = 8
FAR_FIRST = sorted(
    [(x, z, c) for x in range(4) for z in range(4) for c in range(2) if x or z or c],
    key=lambda s: (-min(s[0], 4 - s[0]) - min(s[1], 4 - s[1]), s),
)

COS_TERMS = (
    0.999999009718151, -19.738932854525416, 64.92691787698224,
    -85.24978872544477, 58.68039930519758, -20.879193249375327,
)
SIN_TERMS = (
    6.283184816484557, -41.34156560570182, 81.59907809153451,
    -76.60361308658534, 41.288123420059144, -12.375788874464046,
)


def cos_sin(product, two_lons, inverse):
    turns = jnp.floor(product * inverse + 0.5)
    u = (product - turns * two_lons) * inverse
    z = u * u
    c = jnp.full_like(z, COS_TERMS[-1])
    for term in COS_TERMS[-2::-1]:
        c = c * z + term
    s = jnp.full_like(z, SIN_TERMS[-1])
    for term in SIN_TERMS[-2::-1]:
        s = s * z + term
    return c, s * u


def kernel(waves_s, lons_s, waves_v, spectra, legendre, raw, *scratch):
    names = iter(scratch)
    spec, leg = next(names), next(names)
    partial, bands, from_dn, from_up, sum_dn, sum_up, mine, got, coef, table = (
        [next(names) for _ in GROUPS] for _ in range(10)
    )
    acc, out, m_nat, m_grp, c0, s0, c1, s1 = (next(names) for _ in range(8))
    in_sem, y_send, y_recv, a_send, a_recv, o_send, o_recv, own_sem, line_sem = names

    me = lax.axis_index("wave")
    lat = lax.axis_index("lat")
    up = lax.rem(lat + 1, N_LAT)
    dn = lax.rem(lat + N_LAT - 1, N_LAT)
    opp = lax.rem(lat + 2, N_LAT)
    row = lat * BAND + me

    def most_lons(w):
        first = STRIDE * w + STRIDE - 1
        last = NLAT - 1 - STRIDE * w
        return 20 + 4 * jnp.minimum(first, last)

    def peer(step):
        return jnp.bitwise_and(me + step, N_WAVE - 1)

    def load(chunk, which):
        source, target = ((spectra, spec), (legendre, leg))[which]
        slots = pl.ds(chunk * CHUNK, CHUNK)
        return pltpu.make_async_copy(source.at[slots], target.at[slots], in_sem.at[chunk, which])

    for chunk in range(SLOTS // CHUNK):
        for which in range(2):
            load(chunk, which).start()

    barrier = pltpu.get_barrier_semaphore()
    for other in (up, dn):
        pl.semaphore_signal(
            barrier, inc=1, device_id={"wave": me, "lat": other}, device_id_type=pl.DeviceIdType.MESH
        )

    def shifted(dx, dz, dcore):
        x = jnp.bitwise_and(me // 8 + dx, 3)
        z = jnp.bitwise_and(me // 2 + dz, 3)
        return x * 8 + z * 2 + jnp.bitwise_xor(jnp.bitwise_and(me, 1), dcore)

    plane = [(dx, 0, dcore) for dx in range(4) for dcore in range(2) if dx or dcore]
    line = [(0, dz, 0) for dz in range(1, 4)]
    for shift in plane + line:
        pl.semaphore_signal(
            barrier, inc=1, device_id={"wave": shifted(*shift), "lat": lat},
            device_id_type=pl.DeviceIdType.MESH,
        )

    def tell():
        for shift in line:
            pl.semaphore_signal(
                line_sem, inc=1, device_id={"wave": shifted(*shift), "lat": lat},
                device_id_type=pl.DeviceIdType.MESH,
            )

    def hear():
        pl.semaphore_wait(line_sem, len(line))

    def along_y(g, at, source, target, other):
        return pltpu.make_async_remote_copy(
            src_ref=source, dst_ref=target, send_sem=y_send.at[g, at], recv_sem=y_recv.at[g, at],
            device_id={"wave": me, "lat": other}, device_id_type=pl.DeviceIdType.MESH,
        )

    def y_copies(g):
        half = BAND // 2 * GROUPS[g][1]
        lo, hi = pl.ds(0, half), pl.ds(half, half)
        b = bands[g]
        return (
            along_y(g, 0, b.at[opp, lo], from_dn[g], up),
            along_y(g, 1, b.at[opp, hi], from_up[g], dn),
            along_y(g, 2, b.at[up, hi], sum_dn[g].at[hi], up),
            along_y(g, 3, b.at[dn, lo], sum_up[g].at[lo], dn),
            along_y(g, 4, b.at[up, lo], sum_dn[g].at[lo], up),
            along_y(g, 5, b.at[dn, hi], sum_up[g].at[hi], dn),
        )

    def legendre_sums(g):
        off, size = GROUPS[g]

        def slot(s, carry):
            live = M - waves_s[me * SLOTS + off + s] - lat * DEPTH
            offsets = lax.broadcasted_iota(jnp.int32, (DEPTH, LANES), 0)
            masked = jnp.where(offsets < live, spec[off + s].astype(jnp.float32), 0.0)
            partial[g][pl.ds(pl.multiple_of(s * NLW, NLW), NLW), :] = lax.dot_general(
                leg[off + s], masked.astype(jnp.bfloat16), (((0,), (0,)), ((), ())),
                preferred_element_type=jnp.float32,
            )
            return carry

        def several(i, carry):
            for which in range(2):
                load(off // CHUNK + i, which).wait()
            return lax.fori_loop(0, CHUNK, lambda j, c: slot(i * CHUNK + j, c), carry, unroll=8)

        lax.fori_loop(0, size // CHUNK, several, 0)

    def by_row(g, band):
        size = GROUPS[g][1]

        def pair(i, carry):
            first = band * BAND + 2 * i
            rows = [partial[g][pl.ds(first + j, size, stride=NLW), :] for j in range(2)]
            bands[g][band, pl.ds(pl.multiple_of(i * 2 * size, 2 * size), 2 * size), :] = (
                jnp.concatenate(rows, 0).astype(jnp.bfloat16)
            )
            return carry

        lax.fori_loop(0, BAND // 2, pair, 0, unroll=16)

    def merge(g, band, at, received):
        half = BAND // 2 * GROUPS[g][1]
        step = half // 4

        def part(i, carry):
            rows = pl.ds(pl.multiple_of(at * half + i * step, 32), step)
            other = pl.ds(pl.multiple_of(i * step, 32), step)
            total = bands[g][band, rows, :].astype(jnp.float32) + received[other, :].astype(jnp.float32)
            bands[g][band, rows, :] = total.astype(jnp.bfloat16)
            return carry

        lax.fori_loop(0, 4, part, 0, unroll=4)

    def total(g):
        size = GROUPS[g][1]

        def pair(i, carry):
            rows = pl.ds(pl.multiple_of(i * 2 * size, 2 * size), 2 * size)
            value = bands[g][lat, rows, :].astype(jnp.float32)
            value += sum_dn[g][rows, :].astype(jnp.float32)
            value += sum_up[g][rows, :].astype(jnp.float32)
            mine[g][2 * i] = value[:size].astype(jnp.bfloat16)
            mine[g][2 * i + 1] = value[size:].astype(jnp.bfloat16)
            return carry

        lax.fori_loop(0, BAND // 2, pair, 0, unroll=8)

    def to_row(g, other, sender):
        return pltpu.make_async_remote_copy(
            src_ref=mine[g].at[other], dst_ref=got[g].at[sender],
            send_sem=a_send.at[g], recv_sem=a_recv.at[g],
            device_id={"wave": other, "lat": lat}, device_id_type=pl.DeviceIdType.MESH,
        )

    def all_rows(g):
        first = pl.ds(0, N_WAVE - 1)
        return pltpu.make_async_remote_copy(
            src_ref=mine[g].at[first], dst_ref=got[g].at[first],
            send_sem=a_send.at[g], recv_sem=a_recv.at[g],
            device_id={"wave": peer(1), "lat": lat}, device_id_type=pl.DeviceIdType.MESH,
        )

    def send_rows(g):
        for shift in FAR_FIRST:
            to_row(g, shifted(*shift), me).start()
        got[g][me] = mine[g][me]

    lons = lons_s[row].astype(jnp.float32)
    two = 2.0 * lons

    def reciprocal():
        return 1.0 / jnp.full((8, LANES), two, jnp.float32)

    def phase_tables():
        inverse = reciprocal()

        def spread(r, carry):
            line = waves_v[pl.ds(r, 1), :].astype(jnp.float32)
            m_nat[pl.ds(pl.multiple_of(r * LANES, LANES), LANES), :] = jnp.transpose(
                jnp.broadcast_to(line, (LANES, LANES))
            )
            return carry

        lax.fori_loop(0, M // LANES, spread, 0, unroll=5)

        def regroup(v, carry):
            for off, size in GROUPS:
                m_grp[pl.ds(pl.multiple_of(N_WAVE * off + v * size, 8), size), :] = m_nat[
                    pl.ds(pl.multiple_of(v * SLOTS + off, 8), size), :
                ]
            return carry

        lax.fori_loop(0, N_WAVE, regroup, 0, unroll=4)

        lane = lax.broadcasted_iota(jnp.int32, (8, LANES), 1)
        first = jnp.where(lane < F, BLOCK - 1.0, 3.0 * BLOCK - 1.0).astype(jnp.float32)

        def phases(i, carry):
            for j in range(4):
                rows = pl.ds(pl.multiple_of(i * 32 + j * 8, 8), 8)
                m = m_grp[rows, :]
                weight = jnp.where(m == 0.0, 1.0, jnp.where(2.0 * m < lons, 2.0, 0.0))
                c, s = cos_sin(m * first, two, inverse)
                c0[rows, :] = weight * c
                s0[rows, :] = weight * s
                c, s = cos_sin(m * (4.0 * BLOCK), two, inverse)
                c1[rows, :] = c
                s1[rows, :] = s
            return carry

        lax.fori_loop(0, M // 32, phases, 0, unroll=2)

    def block_tables():
        inverse = reciprocal()
        line = lax.broadcasted_iota(jnp.int32, (8, LANES), 0).astype(jnp.float32)
        for g, (off, size) in enumerate(GROUPS):
            depth = N_WAVE * size

            def columns(i, carry, g=g, off=off, depth=depth):
                base = pl.multiple_of(N_WAVE * off + i * LANES, LANES)
                m = jnp.transpose(m_grp[pl.ds(base, LANES), :])[0:8, :]
                left = pl.ds(pl.multiple_of(i * LANES, LANES), LANES)
                right = pl.ds(pl.multiple_of(depth + i * LANES, LANES), LANES)
                fine = [cos_sin(m * (2.0 * line + 16.0 * h), two, inverse) for h in range(2)]
                fine_c = jnp.concatenate([f[0] for f in fine], 0)
                fine_s = jnp.concatenate([f[1] for f in fine], 0)
                for top in range(0, BLOCK // 16, 8):
                    coarse = m * (32.0 * (line + top) - (BLOCK - 1.0))
                    coarse_c, coarse_s = cos_sin(coarse, two, inverse)
                    for j in range(min(8, BLOCK // 16 - top)):
                        a_c, a_s = coarse_c[j : j + 1], coarse_s[j : j + 1]
                        c = fine_c * a_c - fine_s * a_s
                        s = fine_s * a_c + fine_c * a_s
                        at = 16 * (top + j)
                        table[g][at : at + 16, left] = c.astype(jnp.bfloat16)
                        table[g][at : at + 16, right] = (-s).astype(jnp.bfloat16)
                return carry

            lax.fori_loop(0, depth // LANES, columns, 0)

    def rotate(g):
        off, size = GROUPS[g]
        depth = N_WAVE * size

        def pair(i, carry):
            value = jnp.concatenate(
                [got[g][2 * i + j].astype(jnp.float32) for j in range(2)], 0
            )
            swapped = pltpu.roll(value, F, 1)
            lane = lax.broadcasted_iota(jnp.int32, value.shape, 1)
            real = jnp.where(lane < F, value, swapped)
            imag = jnp.where(lane < F, swapped, value)
            rows = pl.ds(pl.multiple_of(N_WAVE * off + i * 2 * size, 16), 2 * size)
            c, s = c0[rows, :], s0[rows, :]
            a, b = real * c - imag * s, real * s + imag * c
            c, s = c1[rows, :], s1[rows, :]
            at = pl.multiple_of(i * 2 * size, 16)
            for p in range(2 * QUADS):
                columns = slice(LANES * (p % 2), LANES * (p % 2) + LANES)
                coef[g][p // 2, pl.ds(at, 2 * size), columns] = a.astype(jnp.bfloat16)
                coef[g][p // 2, pl.ds(depth + at, 2 * size), columns] = b.astype(jnp.bfloat16)
                if p < 2 * QUADS - 1:
                    a, b = a * c - b * s, a * s + b * c
            return carry

        lax.fori_loop(0, N_WAVE // 2, pair, 0, unroll=4)

    def product(g, quad):
        return jnp.dot(table[g][...], coef[g][quad], preferred_element_type=jnp.float32)

    def to_owner(other, sender):
        return pltpu.make_async_remote_copy(
            src_ref=out.at[other], dst_ref=raw.at[sender],
            send_sem=o_send.at[other], recv_sem=o_recv.at[sender],
            device_id={"wave": other, "lat": lat}, device_id_type=pl.DeviceIdType.MESH,
        )

    def far_first(step):
        return jnp.where(step == 0, 2, jnp.where(step == 1, 3, jnp.where(step == 2, 1, 0)))

    limit = most_lons(row)
    last = len(GROUPS) - 1

    copies = [y_copies(g) for g in range(len(GROUPS))]
    legendre_sums(0)
    by_row(0, opp)
    pl.semaphore_wait(barrier, 2 + len(plane) + len(line))
    copies[0][0].start()
    copies[0][1].start()
    tell()
    by_row(0, up)
    copies[0][2].start()
    by_row(0, dn)
    copies[0][3].start()
    legendre_sums(1)
    by_row(1, opp)
    copies[1][0].start()
    copies[1][1].start()
    copies[0][0].wait_recv()
    merge(0, up, 0, from_dn[0])
    copies[0][4].start()
    copies[0][1].wait_recv()
    merge(0, dn, 1, from_up[0])
    copies[0][5].start()
    by_row(1, up)
    copies[1][2].start()
    by_row(1, dn)
    copies[1][3].start()
    phase_tables()
    copies[1][0].wait_recv()
    merge(1, up, 0, from_dn[1])
    copies[1][4].start()
    copies[1][1].wait_recv()
    merge(1, dn, 1, from_up[1])
    copies[1][5].start()
    by_row(0, lat)
    by_row(1, lat)
    block_tables()
    hear()

    for at in range(2, 6):
        copies[0][at].wait_recv()
    total(0)
    send_rows(0)
    for at in range(2, 6):
        copies[1][at].wait_recv()
    total(1)
    send_rows(1)

    all_rows(0).wait_recv()
    rotate(0)

    def early(quad, carry):
        acc[quad] = product(0, quad)
        return carry

    lax.fori_loop(0, QUADS, early, 0)
    all_rows(1).wait_recv()
    rotate(1)

    def late(step, carry):
        quad = jnp.bitwise_and(me // 8 + far_first(step), QUADS - 1)
        value = acc[quad] + product(1, quad)
        lane = lax.broadcasted_iota(jnp.int32, (HALF, LANES), 1)
        for p in range(2):
            for c in range(2):
                columns = slice(LANES * p, LANES * (p + 1))
                top = value[LONS * c : LONS * c + HALF, columns]
                bottom = value[LONS * c + HALF : LONS * (c + 1), columns]
                even = jnp.where(lane < F, top, pltpu.roll(bottom, F, 1))
                odd = jnp.where(lane < F, pltpu.roll(top, F, 1), bottom)
                out[quad * 8 + 4 * p + c] = even.astype(jnp.bfloat16)
                out[quad * 8 + 4 * p + 2 + c] = odd.astype(jnp.bfloat16)
        for j in range(8):
            other = quad * 8 + j

            @pl.when((other != me) & (other * LONS < limit))
            def _():
                to_owner(other, me).start()

        return carry

    lax.fori_loop(0, QUADS, late, 0)
    keep = pltpu.make_async_copy(out.at[me], raw.at[me], own_sem)
    keep.start()

    def gone(step, carry):
        other = peer(step)

        @pl.when(other * LONS < limit)
        def _():
            to_owner(other, me).wait_send()

        return carry

    lax.fori_loop(1, N_WAVE, gone, 0)
    for g in range(len(GROUPS)):
        all_rows(g).wait_send()
        for copy in copies[g]:
            copy.wait_send()
    def arrived(step, carry):
        sender = jnp.bitwise_and(me // 8 - far_first(step // 8), 3) * 8 + jnp.bitwise_and(me + step, 7)

        @pl.when((me * LONS < most_lons(lat * BAND + sender)) & (sender != me))
        def _():
            to_owner(me, sender).wait_recv()

        return carry

    lax.fori_loop(0, N_WAVE, arrived, 0)
    keep.wait()


def unpack_kernel(lons_s, raw, grid):
    first = lax.axis_index("lat") * BAND
    k = lax.axis_index("wave") * LONS + lax.broadcasted_iota(jnp.int32, (F, LONS), 1)
    for w in range(BAND):
        turned = jnp.transpose(raw[w]).astype(jnp.float32)
        line = jnp.concatenate([turned[:F], turned[F:]], 1)
        grid[w] = jnp.where(k < lons_s[first + w], line, 0.0).astype(jnp.bfloat16)


def local(spectra, legendre, wave_list, cycle_lons):
    bf16, f32 = jnp.bfloat16, jnp.float32
    sizes = [size for _, size in GROUPS]
    scratch = [
        pltpu.VMEM((SLOTS, DEPTH, LANES), bf16),
        pltpu.VMEM((SLOTS, DEPTH, LANES), bf16),
    ]
    scratch += [pltpu.VMEM((n * NLW, LANES), f32) for n in sizes]
    scratch += [pltpu.VMEM((N_LAT, BAND * n, LANES), bf16) for n in sizes]
    for rows in (BAND // 2, BAND // 2, BAND, BAND):
        scratch += [pltpu.VMEM((rows * n, LANES), bf16) for n in sizes]
    scratch += [pltpu.VMEM((BAND, n, LANES), bf16) for n in sizes]
    scratch += [pltpu.VMEM((N_WAVE, n, LANES), bf16) for n in sizes]
    scratch += [pltpu.VMEM((QUADS, 2 * N_WAVE * n, 2 * LANES), bf16) for n in sizes]
    scratch += [pltpu.VMEM((BLOCK, 2 * N_WAVE * n), bf16) for n in sizes]
    scratch += [pltpu.VMEM((QUADS, BLOCK, 2 * LANES), f32)]
    scratch += [pltpu.VMEM((N_WAVE, HALF, LANES), bf16)]
    scratch += [pltpu.VMEM((M, LANES), f32) for _ in range(6)]
    dma = pltpu.SemaphoreType.DMA
    count = len(GROUPS)
    scratch += [dma((SLOTS // CHUNK, 2)), dma((count, 6)), dma((count, 6)), dma((count,))]
    scratch += [dma((count,)), dma((N_WAVE,)), dma((N_WAVE,)), dma]
    scratch += [pltpu.SemaphoreType.REGULAR]

    raw = pl.pallas_call(
        kernel,
        out_shape=jax.ShapeDtypeStruct((BAND, HALF, LANES), bf16),
        in_specs=[
            pl.BlockSpec(memory_space=pltpu.SMEM),
            pl.BlockSpec(memory_space=pltpu.SMEM),
            pl.BlockSpec(memory_space=pltpu.VMEM),
            pl.BlockSpec(memory_space=pl.ANY),
            pl.BlockSpec(memory_space=pl.ANY),
        ],
        out_specs=pl.BlockSpec(memory_space=pl.ANY),
        scratch_shapes=scratch,
        compiler_params=pltpu.CompilerParams(
            collective_id=0, has_side_effects=True, vmem_limit_bytes=56 * 2**20
        ),
    )(wave_list, cycle_lons, wave_list.reshape(M // LANES, LANES), spectra, legendre)
    grid = pl.pallas_call(
        unpack_kernel,
        out_shape=jax.ShapeDtypeStruct((BAND, F, LONS), bf16),
        in_specs=[pl.BlockSpec(memory_space=pltpu.SMEM), pl.BlockSpec(memory_space=pltpu.VMEM)],
        out_specs=pl.BlockSpec(memory_space=pltpu.VMEM),
    )(cycle_lons, raw)
    return jnp.transpose(grid, (0, 2, 1))


def solution(mesh):
    in_specs = (P("wave", "lat", None), P("wave", "lat", None), P(), P())
    out_specs = P("lat", "wave", None)
    return jax.shard_map(local, mesh=mesh, in_specs=in_specs, out_specs=out_specs, check_vma=False)
```

```python
import jax
import jax.numpy as jnp
from jax import lax
from jax.experimental import pallas as pl
from jax.experimental.pallas import tpu as pltpu
from jax.sharding import PartitionSpec as P

M = 1280
F = 64
NLW = 128
NLAT = 2560
STRIDE = 20
NLONP = 5632
N_WAVE = 32
N_LAT = 4

SLOTS = M // N_WAVE
DEPTH = M // N_LAT
BAND = NLW // N_LAT
LONS = NLONP // N_WAVE
HALF = LONS // 2
LANES = 128
BLOCK = 2 * LONS
QUADS = N_WAVE // 8
GROUPS = ((0, 16), (16, 24))
CHUNK = 8
FAR_FIRST = sorted(
    [(x, z, c) for x in range(4) for z in range(4) for c in range(2) if x or z or c],
    key=lambda s: (-min(s[0], 4 - s[0]) - min(s[1], 4 - s[1]), s),
)

COS_TERMS = (
    0.999999009718151, -19.738932854525416, 64.92691787698224,
    -85.24978872544477, 58.68039930519758, -20.879193249375327,
)
SIN_TERMS = (
    6.283184816484557, -41.34156560570182, 81.59907809153451,
    -76.60361308658534, 41.288123420059144, -12.375788874464046,
)


def cos_sin(product, two_lons, inverse):
    turns = jnp.floor(product * inverse + 0.5)
    u = (product - turns * two_lons) * inverse
    z = u * u
    c = jnp.full_like(z, COS_TERMS[-1])
    for term in COS_TERMS[-2::-1]:
        c = c * z + term
    s = jnp.full_like(z, SIN_TERMS[-1])
    for term in SIN_TERMS[-2::-1]:
        s = s * z + term
    return c, s * u


def kernel(waves_s, lons_s, waves_v, spectra, legendre, raw, *scratch):
    names = iter(scratch)
    spec, leg = next(names), next(names)
    partial, bands, from_dn, from_up, sum_dn, sum_up, mine, got, coef, table = (
        [next(names) for _ in GROUPS] for _ in range(10)
    )
    acc, out, m_nat, m_grp, c0, s0, c1, s1 = (next(names) for _ in range(8))
    in_sem, y_send, y_recv, a_send, a_recv, o_send, o_recv, own_sem, line_sem = names

    me = lax.axis_index("wave")
    lat = lax.axis_index("lat")
    up = lax.rem(lat + 1, N_LAT)
    dn = lax.rem(lat + N_LAT - 1, N_LAT)
    opp = lax.rem(lat + 2, N_LAT)
    row = lat * BAND + me

    def most_lons(w):
        first = STRIDE * w + STRIDE - 1
        last = NLAT - 1 - STRIDE * w
        return 20 + 4 * jnp.minimum(first, last)

    def peer(step):
        return jnp.bitwise_and(me + step, N_WAVE - 1)

    def load(chunk, which):
        source, target = ((spectra, spec), (legendre, leg))[which]
        slots = pl.ds(chunk * CHUNK, CHUNK)
        return pltpu.make_async_copy(source.at[slots], target.at[slots], in_sem.at[chunk, which])

    for chunk in range(SLOTS // CHUNK):
        for which in range(2):
            load(chunk, which).start()

    barrier = pltpu.get_barrier_semaphore()
    for other in (up, dn):
        pl.semaphore_signal(
            barrier, inc=1, device_id={"wave": me, "lat": other}, device_id_type=pl.DeviceIdType.MESH
        )

    def shifted(dx, dz, dcore):
        x = jnp.bitwise_and(me // 8 + dx, 3)
        z = jnp.bitwise_and(me // 2 + dz, 3)
        return x * 8 + z * 2 + jnp.bitwise_xor(jnp.bitwise_and(me, 1), dcore)

    plane = [(dx, 0, dcore) for dx in range(4) for dcore in range(2) if dx or dcore]
    line = [(0, dz, 0) for dz in range(1, 4)]
    for shift in plane + line:
        pl.semaphore_signal(
            barrier, inc=1, device_id={"wave": shifted(*shift), "lat": lat},
            device_id_type=pl.DeviceIdType.MESH,
        )

    def tell():
        for shift in line:
            pl.semaphore_signal(
                line_sem, inc=1, device_id={"wave": shifted(*shift), "lat": lat},
                device_id_type=pl.DeviceIdType.MESH,
            )

    def hear():
        pl.semaphore_wait(line_sem, len(line))

    def along_y(g, at, source, target, other):
        return pltpu.make_async_remote_copy(
            src_ref=source, dst_ref=target, send_sem=y_send.at[g, at], recv_sem=y_recv.at[g, at],
            device_id={"wave": me, "lat": other}, device_id_type=pl.DeviceIdType.MESH,
        )

    def y_copies(g):
        half = BAND // 2 * GROUPS[g][1]
        lo, hi = pl.ds(0, half), pl.ds(half, half)
        b = bands[g]
        return (
            along_y(g, 0, b.at[opp, lo], from_dn[g], up),
            along_y(g, 1, b.at[opp, hi], from_up[g], dn),
            along_y(g, 2, b.at[up, hi], sum_dn[g].at[hi], up),
            along_y(g, 3, b.at[dn, lo], sum_up[g].at[lo], dn),
            along_y(g, 4, b.at[up, lo], sum_dn[g].at[lo], up),
            along_y(g, 5, b.at[dn, hi], sum_up[g].at[hi], dn),
        )

    def legendre_sums(g):
        off, size = GROUPS[g]

        def slot(s, carry):
            live = M - waves_s[me * SLOTS + off + s] - lat * DEPTH
            offsets = lax.broadcasted_iota(jnp.int32, (DEPTH, LANES), 0)
            masked = jnp.where(offsets < live, spec[off + s].astype(jnp.float32), 0.0)
            partial[g][pl.ds(pl.multiple_of(s * NLW, NLW), NLW), :] = lax.dot_general(
                leg[off + s], masked.astype(jnp.bfloat16), (((0,), (0,)), ((), ())),
                preferred_element_type=jnp.float32,
            )
            return carry

        def several(i, carry):
            for which in range(2):
                load(off // CHUNK + i, which).wait()
            return lax.fori_loop(0, CHUNK, lambda j, c: slot(i * CHUNK + j, c), carry, unroll=8)

        lax.fori_loop(0, size // CHUNK, several, 0)

    def by_row(g, band):
        size = GROUPS[g][1]

        def pair(i, carry):
            first = band * BAND + 2 * i
            rows = [partial[g][pl.ds(first + j, size, stride=NLW), :] for j in range(2)]
            bands[g][band, pl.ds(pl.multiple_of(i * 2 * size, 2 * size), 2 * size), :] = (
                jnp.concatenate(rows, 0).astype(jnp.bfloat16)
            )
            return carry

        lax.fori_loop(0, BAND // 2, pair, 0, unroll=16)

    def merge(g, band, at, received):
        half = BAND // 2 * GROUPS[g][1]
        step = half // 4

        def part(i, carry):
            rows = pl.ds(pl.multiple_of(at * half + i * step, 32), step)
            other = pl.ds(pl.multiple_of(i * step, 32), step)
            total = bands[g][band, rows, :].astype(jnp.float32) + received[other, :].astype(jnp.float32)
            bands[g][band, rows, :] = total.astype(jnp.bfloat16)
            return carry

        lax.fori_loop(0, 4, part, 0, unroll=4)

    def total(g):
        size = GROUPS[g][1]

        def pair(i, carry):
            rows = pl.ds(pl.multiple_of(i * 2 * size, 2 * size), 2 * size)
            value = bands[g][lat, rows, :].astype(jnp.float32)
            value += sum_dn[g][rows, :].astype(jnp.float32)
            value += sum_up[g][rows, :].astype(jnp.float32)
            mine[g][2 * i] = value[:size].astype(jnp.bfloat16)
            mine[g][2 * i + 1] = value[size:].astype(jnp.bfloat16)
            return carry

        lax.fori_loop(0, BAND // 2, pair, 0, unroll=8)

    def to_row(g, other, sender):
        return pltpu.make_async_remote_copy(
            src_ref=mine[g].at[other], dst_ref=got[g].at[sender],
            send_sem=a_send.at[g], recv_sem=a_recv.at[g],
            device_id={"wave": other, "lat": lat}, device_id_type=pl.DeviceIdType.MESH,
        )

    def all_rows(g):
        first = pl.ds(0, N_WAVE - 1)
        return pltpu.make_async_remote_copy(
            src_ref=mine[g].at[first], dst_ref=got[g].at[first],
            send_sem=a_send.at[g], recv_sem=a_recv.at[g],
            device_id={"wave": peer(1), "lat": lat}, device_id_type=pl.DeviceIdType.MESH,
        )

    def send_rows(g):
        for shift in FAR_FIRST:
            to_row(g, shifted(*shift), me).start()
        got[g][me] = mine[g][me]

    lons = lons_s[row].astype(jnp.float32)
    two = 2.0 * lons

    def reciprocal():
        return 1.0 / jnp.full((8, LANES), two, jnp.float32)

    def phase_tables():
        inverse = reciprocal()

        def spread(r, carry):
            line = waves_v[pl.ds(r, 1), :].astype(jnp.float32)
            m_nat[pl.ds(pl.multiple_of(r * LANES, LANES), LANES), :] = jnp.transpose(
                jnp.broadcast_to(line, (LANES, LANES))
            )
            return carry

        lax.fori_loop(0, M // LANES, spread, 0, unroll=5)

        def regroup(v, carry):
            for off, size in GROUPS:
                m_grp[pl.ds(pl.multiple_of(N_WAVE * off + v * size, 8), size), :] = m_nat[
                    pl.ds(pl.multiple_of(v * SLOTS + off, 8), size), :
                ]
            return carry

        lax.fori_loop(0, N_WAVE, regroup, 0, unroll=4)

        lane = lax.broadcasted_iota(jnp.int32, (8, LANES), 1)
        first = jnp.where(lane < F, BLOCK - 1.0, 3.0 * BLOCK - 1.0).astype(jnp.float32)

        def phases(i, carry):
            for j in range(4):
                rows = pl.ds(pl.multiple_of(i * 32 + j * 8, 8), 8)
                m = m_grp[rows, :]
                weight = jnp.where(m == 0.0, 1.0, jnp.where(2.0 * m < lons, 2.0, 0.0))
                c, s = cos_sin(m * first, two, inverse)
                c0[rows, :] = weight * c
                s0[rows, :] = weight * s
                c, s = cos_sin(m * (4.0 * BLOCK), two, inverse)
                c1[rows, :] = c
                s1[rows, :] = s
            return carry

        lax.fori_loop(0, M // 32, phases, 0, unroll=2)

    def block_tables():
        inverse = reciprocal()
        line = lax.broadcasted_iota(jnp.int32, (8, LANES), 0).astype(jnp.float32)
        for g, (off, size) in enumerate(GROUPS):
            depth = N_WAVE * size

            def columns(i, carry, g=g, off=off, depth=depth):
                base = pl.multiple_of(N_WAVE * off + i * LANES, LANES)
                m = jnp.transpose(m_grp[pl.ds(base, LANES), :])[0:8, :]
                left = pl.ds(pl.multiple_of(i * LANES, LANES), LANES)
                right = pl.ds(pl.multiple_of(depth + i * LANES, LANES), LANES)
                fine = [cos_sin(m * (2.0 * line + 16.0 * h), two, inverse) for h in range(2)]
                fine_c = jnp.concatenate([f[0] for f in fine], 0)
                fine_s = jnp.concatenate([f[1] for f in fine], 0)
                for top in range(0, BLOCK // 16, 8):
                    coarse = m * (32.0 * (line + top) - (BLOCK - 1.0))
                    coarse_c, coarse_s = cos_sin(coarse, two, inverse)
                    for j in range(min(8, BLOCK // 16 - top)):
                        a_c, a_s = coarse_c[j : j + 1], coarse_s[j : j + 1]
                        c = fine_c * a_c - fine_s * a_s
                        s = fine_s * a_c + fine_c * a_s
                        at = 16 * (top + j)
                        table[g][at : at + 16, left] = c.astype(jnp.bfloat16)
                        table[g][at : at + 16, right] = (-s).astype(jnp.bfloat16)
                return carry

            lax.fori_loop(0, depth // LANES, columns, 0)

    def rotate(g):
        off, size = GROUPS[g]
        depth = N_WAVE * size

        def pair(i, carry):
            value = jnp.concatenate(
                [got[g][2 * i + j].astype(jnp.float32) for j in range(2)], 0
            )
            swapped = pltpu.roll(value, F, 1)
            lane = lax.broadcasted_iota(jnp.int32, value.shape, 1)
            real = jnp.where(lane < F, value, swapped)
            imag = jnp.where(lane < F, swapped, value)
            rows = pl.ds(pl.multiple_of(N_WAVE * off + i * 2 * size, 16), 2 * size)
            c, s = c0[rows, :], s0[rows, :]
            a, b = real * c - imag * s, real * s + imag * c
            c, s = c1[rows, :], s1[rows, :]
            at = pl.multiple_of(i * 2 * size, 16)
            for p in range(2 * QUADS):
                columns = slice(LANES * (p % 2), LANES * (p % 2) + LANES)
                coef[g][p // 2, pl.ds(at, 2 * size), columns] = a.astype(jnp.bfloat16)
                coef[g][p // 2, pl.ds(depth + at, 2 * size), columns] = b.astype(jnp.bfloat16)
                if p < 2 * QUADS - 1:
                    a, b = a * c - b * s, a * s + b * c
            return carry

        lax.fori_loop(0, N_WAVE // 2, pair, 0, unroll=4)

    def product(g, quad):
        return jnp.dot(table[g][...], coef[g][quad], preferred_element_type=jnp.float32)

    def to_owner(other, sender):
        return pltpu.make_async_remote_copy(
            src_ref=out.at[other], dst_ref=raw.at[sender],
            send_sem=o_send.at[other], recv_sem=o_recv.at[sender],
            device_id={"wave": other, "lat": lat}, device_id_type=pl.DeviceIdType.MESH,
        )

    def far_first(step):
        return jnp.where(step == 0, 2, jnp.where(step == 1, 3, jnp.where(step == 2, 1, 0)))

    limit = most_lons(row)
    last = len(GROUPS) - 1

    copies = [y_copies(g) for g in range(len(GROUPS))]
    legendre_sums(0)
    by_row(0, opp)
    pl.semaphore_wait(barrier, 2 + len(plane) + len(line))
    copies[0][0].start()
    copies[0][1].start()
    tell()
    by_row(0, up)
    copies[0][2].start()
    by_row(0, dn)
    copies[0][3].start()
    legendre_sums(1)
    by_row(1, opp)
    copies[1][0].start()
    copies[1][1].start()
    copies[0][0].wait_recv()
    merge(0, up, 0, from_dn[0])
    copies[0][4].start()
    copies[0][1].wait_recv()
    merge(0, dn, 1, from_up[0])
    copies[0][5].start()
    by_row(1, up)
    copies[1][2].start()
    by_row(1, dn)
    copies[1][3].start()
    phase_tables()
    copies[1][0].wait_recv()
    merge(1, up, 0, from_dn[1])
    copies[1][4].start()
    copies[1][1].wait_recv()
    merge(1, dn, 1, from_up[1])
    copies[1][5].start()
    by_row(0, lat)
    by_row(1, lat)
    block_tables()
    hear()

    for at in range(2, 6):
        copies[0][at].wait_recv()
    total(0)
    send_rows(0)
    for at in range(2, 6):
        copies[1][at].wait_recv()
    total(1)
    send_rows(1)

    all_rows(0).wait_recv()
    rotate(0)

    def early(quad, carry):
        @pl.when(quad * 8 * LONS < limit)
        def _():
            acc[quad] = product(0, quad)

        return carry

    lax.fori_loop(0, QUADS, early, 0)
    all_rows(1).wait_recv()
    rotate(1)

    def finish(quad):
        value = acc[quad] + product(1, quad)
        lane = lax.broadcasted_iota(jnp.int32, (HALF, LANES), 1)
        for p in range(2):
            for c in range(2):
                columns = slice(LANES * p, LANES * (p + 1))
                top = value[LONS * c : LONS * c + HALF, columns]
                bottom = value[LONS * c + HALF : LONS * (c + 1), columns]
                even = jnp.where(lane < F, top, pltpu.roll(bottom, F, 1))
                odd = jnp.where(lane < F, pltpu.roll(top, F, 1), bottom)
                out[quad * 8 + 4 * p + c] = even.astype(jnp.bfloat16)
                out[quad * 8 + 4 * p + 2 + c] = odd.astype(jnp.bfloat16)
        for j in range(8):
            other = quad * 8 + j

            @pl.when((other != me) & (other * LONS < limit))
            def _():
                to_owner(other, me).start()

    def late(step, carry):
        quad = jnp.bitwise_and(me // 8 + far_first(step), QUADS - 1)

        @pl.when(quad * 8 * LONS < limit)
        def _():
            finish(quad)

        return carry

    lax.fori_loop(0, QUADS, late, 0)
    keep = pltpu.make_async_copy(out.at[me], raw.at[me], own_sem)

    @pl.when(me * LONS < limit)
    def _():
        keep.start()


    def gone(step, carry):
        other = peer(step)

        @pl.when(other * LONS < limit)
        def _():
            to_owner(other, me).wait_send()

        return carry

    lax.fori_loop(1, N_WAVE, gone, 0)
    for g in range(len(GROUPS)):
        all_rows(g).wait_send()
        for copy in copies[g]:
            copy.wait_send()
    def arrived(step, carry):
        sender = jnp.bitwise_and(me // 8 - far_first(step // 8), 3) * 8 + jnp.bitwise_and(me + step, 7)

        @pl.when((me * LONS < most_lons(lat * BAND + sender)) & (sender != me))
        def _():
            to_owner(me, sender).wait_recv()

        return carry

    lax.fori_loop(0, N_WAVE, arrived, 0)

    @pl.when(me * LONS < limit)
    def _():
        keep.wait()


def unpack_kernel(lons_s, raw, grid):
    first = lax.axis_index("lat") * BAND
    k = lax.axis_index("wave") * LONS + lax.broadcasted_iota(jnp.int32, (F, LONS), 1)
    for w in range(BAND):
        turned = jnp.transpose(raw[w]).astype(jnp.float32)
        line = jnp.concatenate([turned[:F], turned[F:]], 1)
        grid[w] = jnp.where(k < lons_s[first + w], line, 0.0).astype(jnp.bfloat16)


def local(spectra, legendre, wave_list, cycle_lons):
    bf16, f32 = jnp.bfloat16, jnp.float32
    sizes = [size for _, size in GROUPS]
    scratch = [
        pltpu.VMEM((SLOTS, DEPTH, LANES), bf16),
        pltpu.VMEM((SLOTS, DEPTH, LANES), bf16),
    ]
    scratch += [pltpu.VMEM((n * NLW, LANES), f32) for n in sizes]
    scratch += [pltpu.VMEM((N_LAT, BAND * n, LANES), bf16) for n in sizes]
    for rows in (BAND // 2, BAND // 2, BAND, BAND):
        scratch += [pltpu.VMEM((rows * n, LANES), bf16) for n in sizes]
    scratch += [pltpu.VMEM((BAND, n, LANES), bf16) for n in sizes]
    scratch += [pltpu.VMEM((N_WAVE, n, LANES), bf16) for n in sizes]
    scratch += [pltpu.VMEM((QUADS, 2 * N_WAVE * n, 2 * LANES), bf16) for n in sizes]
    scratch += [pltpu.VMEM((BLOCK, 2 * N_WAVE * n), bf16) for n in sizes]
    scratch += [pltpu.VMEM((QUADS, BLOCK, 2 * LANES), f32)]
    scratch += [pltpu.VMEM((N_WAVE, HALF, LANES), bf16)]
    scratch += [pltpu.VMEM((M, LANES), f32) for _ in range(6)]
    dma = pltpu.SemaphoreType.DMA
    count = len(GROUPS)
    scratch += [dma((SLOTS // CHUNK, 2)), dma((count, 6)), dma((count, 6)), dma((count,))]
    scratch += [dma((count,)), dma((N_WAVE,)), dma((N_WAVE,)), dma]
    scratch += [pltpu.SemaphoreType.REGULAR]

    raw = pl.pallas_call(
        kernel,
        out_shape=jax.ShapeDtypeStruct((BAND, HALF, LANES), bf16),
        in_specs=[
            pl.BlockSpec(memory_space=pltpu.SMEM),
            pl.BlockSpec(memory_space=pltpu.SMEM),
            pl.BlockSpec(memory_space=pltpu.VMEM),
            pl.BlockSpec(memory_space=pl.ANY),
            pl.BlockSpec(memory_space=pl.ANY),
        ],
        out_specs=pl.BlockSpec(memory_space=pl.ANY),
        scratch_shapes=scratch,
        compiler_params=pltpu.CompilerParams(
            collective_id=0, has_side_effects=True, vmem_limit_bytes=56 * 2**20
        ),
    )(wave_list, cycle_lons, wave_list.reshape(M // LANES, LANES), spectra, legendre)
    grid = pl.pallas_call(
        unpack_kernel,
        out_shape=jax.ShapeDtypeStruct((BAND, F, LONS), bf16),
        in_specs=[pl.BlockSpec(memory_space=pltpu.SMEM), pl.BlockSpec(memory_space=pltpu.VMEM)],
        out_specs=pl.BlockSpec(memory_space=pltpu.VMEM),
    )(cycle_lons, raw)
    return jnp.transpose(grid, (0, 2, 1))


def solution(mesh):
    in_specs = (P("wave", "lat", None), P("wave", "lat", None), P(), P())
    out_specs = P("lat", "wave", None)
    return jax.shard_map(local, mesh=mesh, in_specs=in_specs, out_specs=out_specs, check_vma=False)
```
